32 devices in a mesh: shot: 2 (over y), row: 4 (over x, core), freq: 4 (over z).
Axes of the slice: x: 2, y: 2, z: 4, core: 2. Of those that a mesh axis runs over, the one named last changes fastest.
Arguments:
- source_field: float32 [2, 8, 1024, 1024], P(None, ('shot', 'freq'), 'row'), parts along dimension 1, may hold values from -6 to 6
- receiver_field: float32 [2, 8, 1024, 1024], P(None, ('shot', 'freq'), 'row'), parts along dimension 1, may hold values from -6 to 6
- slowness: float32 [4, 1024, 1024], P('freq', 'row'), may hold values from 0.22 to 0.67
- owner: int32 [4], replicated, may hold values from 0 to 3, each once
- freq_index: int32 [8], P(('shot', 'freq')), parts along dimension 0, may hold values from 0 to 3, each once
Outputs:
- source_out: float32 [2, 8, 1024, 1024], P(None, ('shot', 'freq'), 'row'), parts along dimension 1
- receiver_out: float32 [2, 8, 1024, 1024], P(None, ('shot', 'freq'), 'row'), parts along dimension 1
- image: float32 [4, 1024, 1024], P('shot', 'row', 'freq'), parts along dimension 0
The draws below stay inside these ranges and needn't reach their ends.
There are 2 independent parts, one for each index of `shot`. The reference program is written for one: setup_inputs(seed, part) draws one part's arguments, and reference() takes and returns one part's arrays. A program takes and returns all parts, laid end to end along the dimension named above; an argument that names none is the same for every part. Nothing has to cross between parts.
All inputs are finite; a program needn't handle non-finite values.
Results may differ from the reference program's by a relative error of at most 0.00022.
Values sent between devices are 32-bit elements; how exact they have to be, the bound alone decides.
No kernel may reach another device: no remote copies, remote signals or barrier semaphores. Data moves between devices by JAX's collectives and lax.ppermute only.
A program may use at most 128 MiB of HBM per device.

```python
import math
import jax
import jax.numpy as jnp
from jax import lax

NX = 1024
NY = 1024
NZ = 2
FREQS = 4
SLABS = 4


def level_of(own_key, dims, split, least, top_value):
    level, own = 1.0, jax.random.fold_in(own_key, 6)
    for position, blocks in split:
        heights = jnp.exp(jax.random.uniform(jax.random.fold_in(own, position), (blocks,), jnp.float32, least / len(split), top_value / len(split)))
        level = level * jnp.repeat(heights, dims[position] // blocks).reshape([-1 if axis == position else 1 for axis in range(len(dims))])
    return level


def centred(own_key, extent, scale, reach, split=(), kind=jnp.bfloat16):
    drawn = jax.random.normal(own_key, extent, jnp.float32) * scale
    if len(split) > 0:
        drawn = level_of(own_key, extent, split, -0.22, 0.18) * drawn
    return jnp.clip(drawn, min=-reach, max=reach).astype(kind)


def setup_inputs(seed: int = 0, part: int = 0) -> dict:
    seeds = jax.random.split(jax.random.key(seed), 6)
    part_keys = jax.random.split(jax.random.fold_in(seeds[5], part), 6)
    source_field = centred(part_keys[0], (2, FREQS, NX, NY), 1.0, 6.0, ((1, 4), (2, 4)), jnp.float32)
    receiver_field = centred(part_keys[1], (2, FREQS, NX, NY), 1.0, 6.0, ((1, 4), (2, 4)), jnp.float32)
    slowness = jnp.clip(0.22 + 0.45000002 * jax.random.uniform(seeds[2], (SLABS, NX, NY), jnp.float32) ** level_of(seeds[2], (SLABS, NX, NY), ((0, 4), (1, 4)), -0.2, 0.2), 0.22, 0.67)
    owner = jax.random.permutation(seeds[3], SLABS).astype(jnp.int32)
    freq_index = jax.random.permutation(part_keys[4], FREQS).astype(jnp.int32)
    return dict(source_field=source_field, receiver_field=receiver_field, slowness=slowness, owner=owner, freq_index=freq_index)


dz_km = 0.01
dx_km = 0.0125
ref_slow = 0.5
base_hertz = 3.0
step_hertz = 4.0
taper = 0.5


def wavenumbers(length):
    index = jnp.arange(length, dtype=jnp.int32)
    signed = jnp.where(index * 2 < length, index, index - length)
    return signed.astype(jnp.float32) * (2.0 * math.pi / (length * dx_km))


def reference(source_field, receiver_field, slowness, owner, freq_index):
    kx_all = wavenumbers(NX)
    ky_all = wavenumbers(NY)
    square = kx_all[:, None] ** 2 + ky_all[None, :] ** 2
    kmax = math.pi / dx_km
    damp = jnp.exp(-taper * square / (kmax * kmax))
    omega = 2.0 * math.pi * (base_hertz + step_hertz * freq_index.astype(jnp.float32))
    slabs = [slowness[owner[depth]] for depth in range(NZ)]

    def one_freq(packed):
        omega_one, src_re, src_im, rec_re, rec_im = packed
        source = src_re + 1j * src_im
        receiver = rec_re + 1j * rec_im
        ws0 = omega_one * ref_slow
        vertical = ws0 - 0.5 * square / ws0
        terms = []
        for depth in range(NZ):
            source = jnp.fft.ifft2(jnp.fft.fft2(source) * damp * jnp.exp(1j * dz_km * vertical))
            receiver = jnp.fft.ifft2(jnp.fft.fft2(receiver) * damp * jnp.exp(-1j * dz_km * vertical))
            theta = omega_one * (slabs[depth] - ref_slow) * dz_km
            source = source * jnp.exp(1j * theta)
            receiver = receiver * jnp.exp(-1j * theta)
            terms.append(jnp.real(source) * jnp.real(receiver) + jnp.imag(source) * jnp.imag(receiver))
        return (jnp.real(source), jnp.imag(source), jnp.real(receiver), jnp.imag(receiver), jnp.stack(terms))

    src_re, src_im, rec_re, rec_im, terms = lax.map(
        one_freq, (omega, source_field[0], source_field[1], receiver_field[0], receiver_field[1]))
    image = jnp.sum(terms, axis=0)
    return jnp.stack([src_re, src_im]), jnp.stack([rec_re, rec_im]), image
```

```python
import math

import jax
import jax.numpy as jnp
import numpy as np
from jax import lax
from jax.experimental import pallas as pl
from jax.experimental.pallas import tpu as pltpu
from jax.sharding import PartitionSpec as P

NZ = 2

dz_km = 0.01
dx_km = 0.0125
ref_slow = 0.5
base_hertz = 3.0
step_hertz = 4.0
taper = 0.5

RADIX = 4
LIMIT = 48 * 1024 * 1024
F32 = jnp.float32
BF16 = jnp.bfloat16


def params():
    return pltpu.CompilerParams(vmem_limit_bytes=LIMIT)


def whole(shape):
    return pl.BlockSpec(shape, lambda *_: (0,) * len(shape))


def omega_of(slot):
    return 2.0 * math.pi * (base_hertz + step_hertz * slot.astype(F32))


def add(a, b):
    return (a[0] + b[0], a[1] + b[1])


def sub(a, b):
    return (a[0] - b[0], a[1] - b[1])


def add_i(a, b):
    return (a[0] - b[1], a[1] + b[0])


def sub_i(a, b):
    return (a[0] + b[1], a[1] - b[0])


def spread_blocks(x):
    even, odd = add(x[0], x[2]), add(x[1], x[3])
    plus, minus = sub(x[0], x[2]), sub(x[1], x[3])
    return [add(even, odd), sub_i(plus, minus), sub(even, odd), add_i(plus, minus)]


def join_blocks(y):
    even, odd = add(y[0], y[2]), add(y[1], y[3])
    plus, minus = sub(y[0], y[2]), sub(y[1], y[3])
    return [add(even, odd), add_i(plus, minus), sub(even, odd), sub_i(plus, minus)]


def halves(x):
    high = x.astype(BF16)
    return high, (x - high.astype(F32)).astype(BF16)


def dot(a, b):
    return jnp.dot(a, b, preferred_element_type=F32)


def times_right(x, high, low):
    xr, xi = halves(x[0]), halves(x[1])
    out = []
    for left, right, sign in ((xr, xi, -1), (xi, xr, 1)):
        a = jnp.concatenate([left[0], right[0] * sign], axis=1)
        b = jnp.concatenate([left[1], right[1] * sign], axis=1)
        out.append(dot(a, high) + dot(a, low) + dot(b, high))
    return tuple(out)


def times_left(x, high, low):
    xr, xi = halves(x[0]), halves(x[1])
    size = high.shape[1]
    lead_h = jnp.concatenate([high[:size], high[size:]], axis=1)
    lead_l = jnp.concatenate([low[:size], low[size:]], axis=1)
    out = []
    for left, right, sign in ((xr, xi, -1), (xi, xr, 1)):
        a = jnp.concatenate([left[0], right[0] * sign], axis=0)
        b = jnp.concatenate([left[1], right[1] * sign], axis=0)
        out.append(dot(lead_h, a) + dot(lead_l, a) + dot(lead_h, b))
    return tuple(out)


def convolve(x, high_ref, low_ref, left):
    times = times_left if left else times_right
    x = spread_blocks(x)
    at = [k if left else (RADIX - k) % RADIX for k in range(RADIX)]
    return join_blocks([times(x[k], high_ref[at[k]], low_ref[at[k]]) for k in range(RADIX)])


def phase_parts(theta):
    q = theta * theta
    sin_v = theta * (1.0 + q * (-1 / 6 + q * (1 / 120 + q * (-1 / 5040 + q * (1 / 362880)))))
    cos_v = 1.0 + q * (-0.5 + q * (1 / 24 + q * (-1 / 720 + q * (1 / 40320 - q * (1 / 3628800)))))
    return cos_v, sin_v


def rotate(x, cos_v, sin_v):
    return (x[0] * cos_v - x[1] * sin_v, x[1] * cos_v + x[0] * sin_v)


def cosine_table(length):
    k = np.arange(length // 2)[:, None]
    n = np.arange(length)[None, :]
    table = np.cos(2.0 * math.pi * ((k * n) % length) / length) * np.where(k == 0, 1.0, 2.0)
    return jnp.asarray(table / length, F32)


def propagator(omega, m, length):
    ws0 = omega * ref_slow
    wave = m * (2.0 * math.pi / (length * dx_km))
    square = wave * wave
    kmax = math.pi / dx_km
    damp = jnp.exp(-taper * square / (kmax * kmax))
    phase = dz_km * (0.5 * ws0 - 0.5 * square / ws0)
    return damp * jnp.cos(phase), damp * jnp.sin(phase)


def make_blocks(omega, table_ref, high_ref, low_ref):
    half, length = table_ref.shape
    block = length // RADIX
    m = lax.broadcasted_iota(jnp.int32, (8, half), 1).astype(F32)
    g = propagator(omega, m, length)
    g = tuple(jnp.transpose(part) for part in g)
    lane = lax.broadcasted_iota(jnp.int32, (8, length), 1)
    row = lax.broadcasted_iota(jnp.int32, (8, length), 0)
    last = propagator(omega, jnp.full((8, length), half, F32), length)
    flip = jnp.where(lane % 2 == 0, 1.0, -1.0) / length
    flip = jnp.where(row == 0, flip, 0.0)
    total = [part * flip for part in last]
    for j in range(half // 8):
        here = table_ref[pl.ds(8 * j, 8), :]
        for c in range(2):
            total[c] = total[c] + here * g[c][8 * j : 8 * j + 8, 0:1]
    rows = []
    for c in range(2):
        line = jnp.sum(total[c], axis=0, keepdims=True) * (1.0 / RADIX)
        rows.append(
            pltpu.roll(jnp.broadcast_to(line, (block, length)), 0, 1, stride=1, stride_axis=0)
        )
    parts = [tuple(r[:, e * block : (e + 1) * block] for r in rows) for e in range(RADIX)]
    for k, value in enumerate(join_blocks(parts)):
        for c in range(2):
            high, low = halves(value[c])
            high_ref[k, pl.ds(c * block, block), :] = high
            low_ref[k, pl.ds(c * block, block), :] = low


def pick(ref_value, swap):
    return (ref_value[1], ref_value[0]) if swap else (ref_value[0], ref_value[1])


def store(ref, value, swap):
    ref[0], ref[1] = (value[1], value[0]) if swap else (value[0], value[1])


def first_kernel(form, shift_ref, slot_ref, *refs):
    fields, refs = refs[:RADIX], refs[RADIX:]
    if form:
        table_ref, refs = refs[0], refs[1:]
        outs, (high_ref, low_ref) = refs[:RADIX], refs[RADIX:]

        @pl.when(pl.program_id(0) == 0)
        def _():
            make_blocks(omega_of(slot_ref[0]), table_ref, high_ref, low_ref)

    else:
        (high_ref, low_ref), outs = refs[:2], refs[2:]
    x = [pick(f[:, 0], not form) for f in fields]
    for ref, value in zip(outs, convolve(x, high_ref, low_ref, False)):
        store(ref, value, False)


def first_stage(field, shift, slot, blocks, steps):
    _, _, rows, width = field.shape
    block = width // RADIX
    part = rows // steps
    form = blocks is None
    shape = (RADIX, 2 * block, block)
    specs = [
        pl.BlockSpec((2, 1, part, block), lambda i, sh, _, s=s: (0, 0, i, (sh[0] + s) % RADIX))
        for s in range(RADIX)
    ]
    outs = [jax.ShapeDtypeStruct((2, rows, block), F32)] * RADIX
    out_specs = [pl.BlockSpec((2, part, block), lambda i, *_: (0, i, 0))] * RADIX
    if form:
        more = (cosine_table(width),)
        outs = outs + [jax.ShapeDtypeStruct(shape, BF16)] * 2
        out_specs = out_specs + [whole(shape)] * 2
    else:
        more = tuple(blocks)
    got = pl.pallas_call(
        lambda *refs: first_kernel(form, *refs),
        grid_spec=pltpu.PrefetchScalarGridSpec(
            num_scalar_prefetch=2,
            grid=(steps,),
            in_specs=specs + [whole(a.shape) for a in more],
            out_specs=out_specs,
        ),
        out_shape=outs,
        compiler_params=params(),
        cost_estimate=pl.CostEstimate(flops=2 * 10**9, bytes_accessed=6 * 10**6, transcendentals=0),
        name="along_y_first_s" if form else "along_y_first_r",
    )(shift, slot, *[field] * RADIX, *more)
    return (got[:RADIX], tuple(got[RADIX:])) if form else (got, blocks)


def middle_kernel(count, with_image, *refs):
    fields, refs = refs[:RADIX], refs[RADIX:]
    cos_ref, sin_ref, high_ref, low_ref = refs[:4]
    refs = refs[4:]
    if with_image:
        other_ref, refs = refs[0], refs[1:]
    outs, extra = refs[: RADIX * count], refs[RADIX * count]
    x = convolve([pick(f, False) for f in fields], high_ref, low_ref, True)
    x = [rotate(x[s], cos_ref[s], sin_ref[s]) for s in range(RADIX)]
    for s in range(RADIX):
        if with_image:
            extra[s] = other_ref[s, 0] * x[s][1] + other_ref[s, 1] * x[s][0]
        else:
            extra[s, 0] = x[s][0]
            extra[s, 1] = x[s][1]
    x = convolve(x, high_ref, low_ref, True)
    part = x[0][0].shape[0] // count
    for s in range(RADIX):
        for c in range(count):
            value = tuple(v[c * part : (c + 1) * part] for v in x[s])
            store(outs[s * count + c], value, False)


def middle_stage(fields, phases, blocks, count, other):
    _, rows, cols = fields[0].shape
    with_image = other is not None
    piece = jax.ShapeDtypeStruct((2, rows // count, cols), F32)
    extra = (RADIX, rows, cols) if with_image else (RADIX, 2, rows, cols)
    args = list(fields) + list(phases) + list(blocks) + ([other] if with_image else [])
    outs = [piece] * (RADIX * count) + [jax.ShapeDtypeStruct(extra, F32)]
    got = pl.pallas_call(
        lambda *refs: middle_kernel(count, with_image, *refs),
        in_specs=[whole(a.shape) for a in args],
        out_specs=[whole(o.shape) for o in outs],
        out_shape=outs,
        compiler_params=params(),
        cost_estimate=pl.CostEstimate(flops=4 * 10**9, bytes_accessed=12 * 10**6, transcendentals=0),
        name="along_x_r" if with_image else "along_x_s",
    )(*args)
    pieces = [[got[s * count + c] for s in range(RADIX)] for c in range(count)]
    return pieces, got[-1]


def last_kernel(with_image, shift_ref, slot_ref, place_ref, *refs):
    fields, refs = refs[:RADIX], refs[RADIX:]
    slab_ref, high_ref, low_ref = refs[:3]
    refs = refs[3:]
    if with_image:
        other_ref = refs[0]
        out_ref, terms, line = refs[-(RADIX + 2)], refs[-(RADIX + 1) : -1], refs[-1]
    else:
        out_ref = refs[-1]
    block = fields[0].shape[2]
    omega = omega_of(slot_ref[0])
    x = convolve([pick(f, False) for f in fields], high_ref, low_ref, False)
    for s in range(RADIX):
        at = pl.ds(pl.multiple_of(lax.rem(shift_ref[0] + s, RADIX) * block, block), block)
        theta = omega * (slab_ref[:, at] - ref_slow) * dz_km
        value = rotate(x[s], *phase_parts(theta))
        if with_image:
            line[:, at] = other_ref[0, 0, :, at] * value[1] + other_ref[1, 0, :, at] * value[0]
            value = (value[1], value[0])
        out_ref[0, 0, :, at] = value[0]
        out_ref[1, 0, :, at] = value[1]
    if with_image:
        count = len(terms)
        part = line.shape[1] // count
        for t in range(count):
            at = pl.ds(pl.multiple_of(lax.rem(place_ref[0] + t, count) * part, part), part)
            terms[t][...] = line[:, at]


def last_stage(fields, slab, blocks, shift, slot, place, start, rows, other, held):
    _, part, block = fields[0].shape
    width = block * RADIX
    with_image = other is not None
    row = start // part
    wide = pl.BlockSpec((2, 1, part, width), lambda i, *_: (0, 0, row, 0))
    args = list(fields) + [slab] + list(blocks)
    specs = [whole(f.shape) for f in fields]
    specs += [pl.BlockSpec((part, width), lambda i, *_: (row, 0))]
    specs += [whole(b.shape) for b in blocks]
    outs = [jax.ShapeDtypeStruct((2, 1, rows, width), F32)]
    out_specs = [wide]
    scratch = []
    if with_image:
        args.append(other)
        specs.append(wide)
        cols = width // RADIX
        outs += [jax.ShapeDtypeStruct((part, cols), F32)] * RADIX
        out_specs += [whole((part, cols))] * RADIX
        scratch = [pltpu.VMEM((part, width), F32)]
    alias = {}
    if held is not None:
        alias = {3 + len(args): 0}
        args.append(held)
        specs.append(pl.BlockSpec(memory_space=pl.ANY))
    got = pl.pallas_call(
        lambda *refs: last_kernel(with_image, *refs),
        grid_spec=pltpu.PrefetchScalarGridSpec(
            num_scalar_prefetch=3,
            grid=(1,),
            in_specs=specs,
            out_specs=out_specs,
            scratch_shapes=scratch,
        ),
        out_shape=outs,
        input_output_aliases=alias,
        compiler_params=params(),
        cost_estimate=pl.CostEstimate(flops=10**9, bytes_accessed=6 * 10**6, transcendentals=0),
        name="along_y_last_r" if with_image else "along_y_last_s",
    )(shift, slot, place, *args)
    return got[0], got[1:]


def phase_kernel(slot_ref, place_ref, *refs):
    pieces, (cos_ref, sin_ref) = refs[:-2], refs[-2:]
    count = len(pieces)
    sub_rows = pieces[0].shape[1]
    omega = omega_of(slot_ref[0])
    for t in range(count):
        at = pl.ds(pl.multiple_of(lax.rem(place_ref[0] + t, count) * sub_rows, 8), sub_rows)
        for s in range(RADIX):
            theta = omega * (pieces[t][s] - ref_slow) * dz_km
            cos_ref[s, at, :], sin_ref[s, at, :] = phase_parts(theta)


def phase_stage(pieces, slot, place):
    _, sub_rows, cols = pieces[0].shape
    shape = (RADIX, sub_rows * len(pieces), cols)
    return pl.pallas_call(
        phase_kernel,
        grid_spec=pltpu.PrefetchScalarGridSpec(
            num_scalar_prefetch=2,
            grid=(1,),
            in_specs=[whole(p.shape) for p in pieces],
            out_specs=[whole(shape)] * 2,
        ),
        out_shape=[jax.ShapeDtypeStruct(shape, F32)] * 2,
        compiler_params=params(),
        cost_estimate=pl.CostEstimate(flops=10**7, bytes_accessed=3 * 10**6, transcendentals=0),
        name="phases",
    )(slot, place, *pieces)


def image_kernel(chunks, early_ref, *refs):
    out_ref = refs[-1]
    count = (len(refs) - 1) // chunks
    out_ref[0] = early_ref[...]
    part = refs[0].shape[0]
    for c in range(chunks):
        mine = refs[c * count : (c + 1) * count]
        total = mine[0][...]
        for ref in mine[1:]:
            total = total + ref[...]
        out_ref[1, pl.ds(c * part, part), :] = total


def image_stage(early, groups):
    rows, cols = early.shape
    args = [early] + [piece for group in groups for piece in group]
    return pl.pallas_call(
        lambda *refs: image_kernel(len(groups), *refs),
        out_shape=jax.ShapeDtypeStruct((NZ, rows, cols), F32),
        compiler_params=params(),
        cost_estimate=pl.CostEstimate(flops=10**6, bytes_accessed=3 * 10**6, transcendentals=0),
        name="image_sum",
    )(*args)


def shifted(value, axis, step):
    count = lax.axis_size(axis)
    return lax.ppermute(value, axis, [((i + step) % count, i) for i in range(count)])


def swap_slots(pieces, axis):
    count = len(pieces)
    sent = [lax.ppermute(pieces[s], axis, [(i, (i + s) % count) for i in range(count)]) for s in range(1, count)]
    return [pieces[0]] + [sent[count - s - 1] for s in range(1, count)]


def gather_slots(piece, axis):
    return [piece] + [shifted(piece, axis, s) for s in range(1, lax.axis_size(axis))]


CHUNKS = 2


def body(source_field, receiver_field, slowness, owner, freq_index):
    rows, width = source_field.shape[2:]
    row_count = lax.axis_size("row")
    freq_count = lax.axis_size("freq")
    row_at = lax.axis_index("row")
    place = lax.axis_index("freq")[None]
    slot = freq_index
    ringed = row_count == RADIX and freq_count == RADIX and slowness.shape[0] == 1
    shift = row_at[None] if ringed else jnp.zeros((1,), jnp.int32)
    if not ringed:
        return general(source_field, receiver_field, slowness, owner, slot, shift, place)
    block = width // RADIX
    sub_rows = rows // RADIX

    s_first, blocks = first_stage(source_field, shift, slot, None, 2)
    s_mid = swap_slots(s_first, "row")
    slab = slowness[0].reshape(RADIX, sub_rows, width)
    mine = [lax.dynamic_index_in_dim(slab, (place[0] + t) % RADIX, 0, keepdims=False) for t in range(RADIX)]
    shares = swap_slots(mine, "freq")
    r_first, _ = first_stage(receiver_field, shift, slot, blocks, 2)
    r_mid = swap_slots(r_first, "row")
    stack = jnp.stack(shares)
    early, late = [lax.dynamic_index_in_dim(stack, (owner[z] - place[0]) % RADIX, 0, keepdims=False) for z in range(NZ)]
    turned = early.reshape(sub_rows, RADIX, block)
    turned = [lax.dynamic_index_in_dim(turned, (row_at + s) % RADIX, 1, keepdims=False) for s in range(RADIX)]
    turned = jnp.stack(swap_slots(turned, "row"))
    phases = phase_stage(gather_slots(turned, "freq"), slot, place)
    late = lax.all_gather(late, "freq", axis=0, tiled=True)

    s_pieces, s_held = middle_stage(s_mid, phases, blocks, 1, None)
    s_last = swap_slots(s_pieces[0], "row")
    r_pieces, term = middle_stage(r_mid, phases, blocks, CHUNKS, s_held)
    r_last = [swap_slots(p, "row") for p in r_pieces]
    first_image = lax.psum_scatter(term, "freq", scatter_dimension=0, tiled=False)
    pairs = []
    for r in range(RADIX):
        for f in range(RADIX):
            pairs.append((r * RADIX + f, ((r + f) % RADIX) * RADIX + r))
    first_image = lax.ppermute(first_image, ("row", "freq"), pairs)

    source_out, _ = last_stage(s_last, late, blocks, shift, slot, place, 0, rows, None, None)
    receiver_out, groups = None, []
    for c in range(CHUNKS):
        receiver_out, terms = last_stage(
            r_last[c], late, blocks, shift, slot, place, c * (rows // CHUNKS), rows, source_out, receiver_out
        )
        groups.append(swap_slots(terms, "freq"))
    return (source_out, receiver_out, image_stage(first_image, groups))


def general(source_field, receiver_field, slowness, owner, slot, shift, place):
    rows, width = source_field.shape[2:]
    slab_dev = slowness.shape[0]
    slabs = []
    for depth in range(NZ):
        chosen = owner[depth]
        kept = lax.dynamic_index_in_dim(slowness, chosen % slab_dev, 0, keepdims=False)
        slabs.append(lax.psum(jnp.where(place[0] == chosen // slab_dev, kept, 0.0), "freq"))
    s_first, blocks = first_stage(source_field, shift, slot, None, 1)
    r_first, _ = first_stage(receiver_field, shift, slot, blocks, 1)

    def to_columns(pieces):
        whole_rows = jnp.concatenate(pieces, axis=2)
        return lax.all_to_all(whole_rows, "row", split_axis=2, concat_axis=1, tiled=True)

    def to_rows(pieces):
        whole_cols = jnp.concatenate(pieces, axis=1)
        return lax.all_to_all(whole_cols, "row", split_axis=1, concat_axis=2, tiled=True)

    s_mid = jnp.split(to_columns(s_first), RADIX, axis=1)
    r_mid = jnp.split(to_columns(r_first), RADIX, axis=1)
    turned = lax.all_to_all(slabs[0], "row", split_axis=1, concat_axis=0, tiled=True)
    theta = omega_of(slot[0]) * (turned - ref_slow) * dz_km
    theta = theta.reshape(RADIX, -1, theta.shape[1])
    phases = (jnp.cos(theta), jnp.sin(theta))
    s_pieces, s_held = middle_stage(s_mid, phases, blocks, 1, None)
    r_pieces, term = middle_stage(r_mid, phases, blocks, 1, s_held)
    s_last = jnp.split(to_rows(s_pieces[0]), RADIX, axis=2)
    r_last = jnp.split(to_rows(r_pieces[0]), RADIX, axis=2)
    source_out, _ = last_stage(s_last, slabs[1], blocks, shift, slot, shift, 0, rows, None, None)
    receiver_out, terms = last_stage(
        r_last, slabs[1], blocks, shift, slot, shift, 0, rows, source_out, None
    )
    term = term.reshape(-1, term.shape[2])
    images = [lax.all_to_all(term, "row", split_axis=0, concat_axis=1, tiled=True)]
    images.append(jnp.concatenate(terms, axis=1))
    parts = [lax.psum_scatter(t, "freq", scatter_dimension=1, tiled=True) for t in images]
    return (source_out, receiver_out, jnp.stack(parts))


def solution(mesh):
    in_specs = (
        P(None, ("shot", "freq"), "row", None),
        P(None, ("shot", "freq"), "row", None),
        P("freq", "row", None),
        P(),
        P(("shot", "freq")),
    )
    out_specs = (
        P(None, ("shot", "freq"), "row", None),
        P(None, ("shot", "freq"), "row", None),
        P("shot", "row", "freq"),
    )
    return jax.shard_map(body, mesh=mesh, in_specs=in_specs, out_specs=out_specs, check_vma=False)
```

```python
import math

import jax
import jax.numpy as jnp
import numpy as np
from jax import lax
from jax.experimental import pallas as pl
from jax.experimental.pallas import tpu as pltpu
from jax.sharding import PartitionSpec as P

NZ = 2

dz_km = 0.01
dx_km = 0.0125
ref_slow = 0.5
base_hertz = 3.0
step_hertz = 4.0
taper = 0.5

RADIX = 4
BRIEF = pl.CostEstimate(flops=1000, bytes_accessed=1000, transcendentals=0)
LONG = pl.CostEstimate(flops=10**11, bytes_accessed=10**7, transcendentals=0)
LIMIT = 20 * 1024 * 1024
F32 = jnp.float32
ANY = pl.BlockSpec(memory_space=pl.ANY)
BF16 = jnp.bfloat16


def params():
    return pltpu.CompilerParams(vmem_limit_bytes=LIMIT)


def whole(shape):
    return pl.BlockSpec(shape, lambda *_: (0,) * len(shape))


def far(arrays):
    return [pltpu.with_memory_space_constraint(a, pltpu.HBM) for a in arrays]


def omega_of(slot):
    return 2.0 * math.pi * (base_hertz + step_hertz * slot.astype(F32))


def add(a, b):
    return (a[0] + b[0], a[1] + b[1])


def sub(a, b):
    return (a[0] - b[0], a[1] - b[1])


def add_i(a, b):
    return (a[0] - b[1], a[1] + b[0])


def sub_i(a, b):
    return (a[0] + b[1], a[1] - b[0])


def spread_blocks(x):
    even, odd = add(x[0], x[2]), add(x[1], x[3])
    plus, minus = sub(x[0], x[2]), sub(x[1], x[3])
    return [add(even, odd), sub_i(plus, minus), sub(even, odd), add_i(plus, minus)]


def join_blocks(y):
    even, odd = add(y[0], y[2]), add(y[1], y[3])
    plus, minus = sub(y[0], y[2]), sub(y[1], y[3])
    return [add(even, odd), add_i(plus, minus), sub(even, odd), sub_i(plus, minus)]


def halves(x):
    high = x.astype(BF16)
    return high, (x - high.astype(F32)).astype(BF16)


def dot(a, b):
    return jnp.dot(a, b, preferred_element_type=F32)


def times_right(x, high, low):
    xr, xi = halves(x[0]), halves(x[1])
    out = []
    for left, right, sign in ((xr, xi, -1), (xi, xr, 1)):
        a = jnp.concatenate([left[0], right[0] * sign], axis=1)
        b = jnp.concatenate([left[1], right[1] * sign], axis=1)
        out.append(dot(a, high) + dot(a, low) + dot(b, high))
    return tuple(out)


def times_left(x, high, low):
    xr, xi = halves(x[0]), halves(x[1])
    size = high.shape[1]
    lead_h = jnp.concatenate([high[:size], high[size:]], axis=1)
    lead_l = jnp.concatenate([low[:size], low[size:]], axis=1)
    out = []
    for left, right, sign in ((xr, xi, -1), (xi, xr, 1)):
        a = jnp.concatenate([left[0], right[0] * sign], axis=0)
        b = jnp.concatenate([left[1], right[1] * sign], axis=0)
        out.append(dot(lead_h, a) + dot(lead_l, a) + dot(lead_h, b))
    return tuple(out)


def block_of(me, slot):
    return lax.bitwise_xor(me, slot)


def convolve(x, high_ref, low_ref, left, me):
    times = times_left if left else times_right
    x = spread_blocks(x)
    flip = lax.bitwise_and(me, 1) * 2
    y = []
    for k in range(RADIX):
        at = k if left else (RADIX - k) % RADIX
        if k % 2 == 1:
            at = lax.bitwise_xor(flip, at)
        y.append(times(x[k], high_ref[at], low_ref[at]))
    return join_blocks(y)


def phase_parts(theta):
    q = theta * theta
    sin_v = theta * (1.0 + q * (-1 / 6 + q * (1 / 120 + q * (-1 / 5040 + q * (1 / 362880)))))
    cos_v = 1.0 + q * (-0.5 + q * (1 / 24 + q * (-1 / 720 + q * (1 / 40320 - q * (1 / 3628800)))))
    return cos_v, sin_v


def rotate(x, cos_v, sin_v):
    return (x[0] * cos_v - x[1] * sin_v, x[1] * cos_v + x[0] * sin_v)


def cosine_table(length):
    k = np.arange(length // 2)[:, None]
    n = np.arange(length)[None, :]
    table = np.cos(2.0 * math.pi * ((k * n) % length) / length) * np.where(k == 0, 1.0, 2.0)
    return jnp.asarray(table / length, F32)


def propagator(omega, m, length):
    ws0 = omega * ref_slow
    wave = m * (2.0 * math.pi / (length * dx_km))
    square = wave * wave
    kmax = math.pi / dx_km
    damp = jnp.exp(-taper * square / (kmax * kmax))
    phase = dz_km * (0.5 * ws0 - 0.5 * square / ws0)
    return damp * jnp.cos(phase), damp * jnp.sin(phase)


def make_blocks(omega, table_ref, high_ref, low_ref):
    half, length = table_ref.shape
    block = length // RADIX
    m = lax.broadcasted_iota(jnp.int32, (8, half), 1).astype(F32)
    g = propagator(omega, m, length)
    g = tuple(jnp.transpose(part) for part in g)
    lane = lax.broadcasted_iota(jnp.int32, (8, length), 1)
    row = lax.broadcasted_iota(jnp.int32, (8, length), 0)
    last = propagator(omega, jnp.full((8, length), half, F32), length)
    flip = jnp.where(lane % 2 == 0, 1.0, -1.0) / length
    flip = jnp.where(row == 0, flip, 0.0)
    total = [part * flip for part in last]
    for j in range(half // 8):
        here = table_ref[pl.ds(8 * j, 8), :]
        for c in range(2):
            total[c] = total[c] + here * g[c][8 * j : 8 * j + 8, 0:1]
    rows = []
    for c in range(2):
        line = jnp.sum(total[c], axis=0, keepdims=True) * (1.0 / RADIX)
        rows.append(
            pltpu.roll(jnp.broadcast_to(line, (block, length)), 0, 1, stride=1, stride_axis=0)
        )
    parts = [tuple(r[:, e * block : (e + 1) * block] for r in rows) for e in range(RADIX)]
    for k, value in enumerate(join_blocks(parts)):
        for c in range(2):
            high, low = halves(value[c])
            high_ref[k, pl.ds(c * block, block), :] = high
            low_ref[k, pl.ds(c * block, block), :] = low


def pick(ref_value, swap):
    return (ref_value[1], ref_value[0]) if swap else (ref_value[0], ref_value[1])


def store(ref, value, swap):
    ref[0], ref[1] = (value[1], value[0]) if swap else (value[0], value[1])


def first_kernel(form, waits, shift_ref, slot_ref, *refs):
    fields, refs = refs[:RADIX], refs[RADIX:]
    if waits:
        refs = refs[waits:]
    if form:
        table_ref, refs = refs[0], refs[1:]
        outs, (high_ref, low_ref) = refs[:RADIX], refs[RADIX:]

        @pl.when(pl.program_id(0) == 0)
        def _():
            make_blocks(omega_of(slot_ref[0]), table_ref, high_ref, low_ref)

    else:
        (high_ref, low_ref), outs = refs[:2], refs[2:]
    x = [pick(f[:, 0], not form) for f in fields]
    for ref, value in zip(outs, convolve(x, high_ref, low_ref, False, shift_ref[0])):
        store(ref, value, False)


def first_stage(field, shift, slot, blocks, steps, after=()):
    _, _, rows, width = field.shape
    block = width // RADIX
    part = rows // steps
    form = blocks is None
    shape = (RADIX, 2 * block, block)
    specs = [
        pl.BlockSpec((2, 1, part, block), lambda i, sh, _, s=s: (0, 0, i, block_of(sh[0], s)))
        for s in range(RADIX)
    ]
    outs = [pltpu.HBM((2, rows, block), F32)] * RADIX
    out_specs = [pl.BlockSpec((2, part, block), lambda i, *_: (0, i, 0))] * RADIX
    if form:
        more = (cosine_table(width),)
        outs = outs + [jax.ShapeDtypeStruct(shape, BF16)] * 2
        out_specs = out_specs + [whole(shape)] * 2
    else:
        more = tuple(blocks)
    got = pl.pallas_call(
        lambda *refs: first_kernel(form, len(after), *refs),
        grid_spec=pltpu.PrefetchScalarGridSpec(
            num_scalar_prefetch=2,
            grid=(steps,),
            in_specs=specs + [ANY] * len(after) + [whole(a.shape) for a in more],
            out_specs=out_specs,
        ),
        out_shape=outs,
        compiler_params=params(),
        cost_estimate=LONG,
        name="along_y_first_s" if form else "along_y_first_r",
    )(shift, slot, *[field] * RADIX, *far(after), *more)
    return (got[:RADIX], tuple(got[RADIX:])) if form else (got, blocks)


def half_kernel(shift_ref, *refs):
    fields, (high_ref, low_ref, out_ref) = refs[:RADIX], refs[RADIX:]
    x = convolve([pick(f, False) for f in fields], high_ref, low_ref, True, shift_ref[0])
    for s in range(RADIX):
        store(out_ref.at[s], x[s], False)


def half_stage(fields, blocks, shift):
    _, rows, cols = fields[0].shape
    args = list(fields) + list(blocks)
    shape = (RADIX, 2, rows, cols)
    return pl.pallas_call(
        half_kernel,
        grid_spec=pltpu.PrefetchScalarGridSpec(
            num_scalar_prefetch=1,
            grid=(1,),
            in_specs=[whole(a.shape) for a in args],
            out_specs=whole(shape),
        ),
        out_shape=jax.ShapeDtypeStruct(shape, F32),
        compiler_params=params(),
        cost_estimate=LONG,
        name="along_x_s_first",
    )(shift, *far(fields), *blocks)


def middle_kernel(count, with_image, waits, shift_ref, *refs):
    if with_image:
        fields, refs = refs[:RADIX], refs[RADIX:]
        other_ref, refs = refs[0], refs[1:]
    else:
        half_ref, refs = refs[0], refs[1:]
    cos_ref, sin_ref, high_ref, low_ref = refs[:4]
    refs = refs[4 + waits :]
    outs, extra = refs[: RADIX * count], refs[RADIX * count :]
    if with_image:
        x = convolve([pick(f, False) for f in fields], high_ref, low_ref, True, shift_ref[0])
    else:
        x = [pick(half_ref.at[s], False) for s in range(RADIX)]
    x = [rotate(x[s], cos_ref[s], sin_ref[s]) for s in range(RADIX)]
    for s in range(RADIX):
        if with_image:
            extra[0][s] = other_ref[s, 0] * x[s][1] + other_ref[s, 1] * x[s][0]
        else:
            store(extra[0].at[s], x[s], False)
    x = convolve(x, high_ref, low_ref, True, shift_ref[0])
    part = x[0][0].shape[0] // count
    for s in range(RADIX):
        for c in range(count):
            value = tuple(v[c * part : (c + 1) * part] for v in x[s])
            store(outs[s * count + c], value, False)


def middle_stage(fields, phases, blocks, shift, count, other, after=()):
    with_image = other is not None
    _, rows, cols = phases[0].shape
    piece = pltpu.HBM((2, rows // count, cols), F32)
    fields = far(fields) if with_image else fields
    extra = (RADIX, rows, cols) if with_image else (RADIX, 2, rows, cols)
    args = list(fields) + ([other] if with_image else []) + list(phases) + list(blocks)
    outs = [piece] * (RADIX * count) + [jax.ShapeDtypeStruct(extra, F32)]
    got = pl.pallas_call(
        lambda *refs: middle_kernel(count, with_image, len(after), *refs),
        grid_spec=pltpu.PrefetchScalarGridSpec(
            num_scalar_prefetch=1,
            grid=(1,),
            in_specs=[whole(a.shape) for a in args] + [ANY] * len(after),
            out_specs=[whole(o.shape) for o in outs],
        ),
        out_shape=outs,
        compiler_params=params(),
        cost_estimate=LONG,
        name="along_x_r" if with_image else "along_x_s_second",
    )(shift, *args, *far(after))
    pieces = [[got[s * count + c] for s in range(RADIX)] for c in range(count)]
    return pieces, got[-1]


def last_kernel(with_image, shift_ref, slot_ref, place_ref, *refs):
    fields, refs = refs[:RADIX], refs[RADIX:]
    slab_ref, high_ref, low_ref = refs[:3]
    refs = refs[3:]
    if with_image:
        other_ref = refs[0]
        out_ref, terms, line = refs[-(RADIX + 2)], refs[-(RADIX + 1) : -1], refs[-1]
    else:
        out_ref = refs[-1]
    block = fields[0].shape[2]
    omega = omega_of(slot_ref[0])
    x = convolve([pick(f, False) for f in fields], high_ref, low_ref, False, shift_ref[0])
    for s in range(RADIX):
        at = pl.ds(pl.multiple_of(block_of(shift_ref[0], s) * block, block), block)
        theta = omega * (slab_ref[:, at] - ref_slow) * dz_km
        value = rotate(x[s], *phase_parts(theta))
        if with_image:
            line[:, at] = other_ref[0, 0, :, at] * value[1] + other_ref[1, 0, :, at] * value[0]
            value = (value[1], value[0])
        out_ref[0, 0, :, at] = value[0]
        out_ref[1, 0, :, at] = value[1]
    if with_image:
        count = len(terms)
        part = line.shape[1] // count
        for t in range(count):
            at = pl.ds(pl.multiple_of(lax.rem(place_ref[0] + t, count) * part, part), part)
            terms[t][...] = line[:, at]


def last_stage(fields, slab, blocks, shift, slot, place, start, rows, other, held):
    _, part, block = fields[0].shape
    width = block * RADIX
    with_image = other is not None
    row = start // part
    wide = pl.BlockSpec((2, 1, part, width), lambda i, *_: (0, 0, row, 0))
    args = far(fields) + [slab] + list(blocks)
    specs = [whole(f.shape) for f in fields]
    specs += [pl.BlockSpec((part, width), lambda i, *_: (row, 0))]
    specs += [whole(b.shape) for b in blocks]
    outs = [jax.ShapeDtypeStruct((2, 1, rows, width), F32)]
    out_specs = [wide]
    scratch = []
    if with_image:
        args += far([other])
        specs.append(wide)
        cols = width // RADIX
        outs += [jax.ShapeDtypeStruct((part, cols), F32)] * RADIX
        out_specs += [whole((part, cols))] * RADIX
        scratch = [pltpu.VMEM((part, width), F32)]
    alias = {}
    if held is not None:
        alias = {3 + len(args): 0}
        args += far([held])
        specs.append(ANY)
    got = pl.pallas_call(
        lambda *refs: last_kernel(with_image, *refs),
        grid_spec=pltpu.PrefetchScalarGridSpec(
            num_scalar_prefetch=3,
            grid=(1,),
            in_specs=specs,
            out_specs=out_specs,
            scratch_shapes=scratch,
        ),
        out_shape=outs,
        input_output_aliases=alias,
        compiler_params=params(),
        cost_estimate=LONG,
        name="along_y_last_r" if with_image else "along_y_last_s",
    )(shift, slot, place, *args)
    return got[0], got[1:]


def cut_kernel(shift_ref, shot_ref, place_ref, owner_ref, slab_ref, *outs):
    part, block = outs[0].shape[1:]
    for t in range(RADIX):
        row = 2 * lax.rem(place_ref[0] + t, RADIX) + shot_ref[0]
        rows = pl.ds(pl.multiple_of(row * part, part), part)
        for s in range(RADIX):
            cols = pl.ds(pl.multiple_of(block_of(shift_ref[0], s) * block, block), block)
            outs[s][t] = slab_ref[0, rows, cols]
    kept = (owner_ref[NZ - 1] == place_ref[0]).astype(F32)
    outs[-1][...] = slab_ref[0] * kept


def cut_stage(slowness, shift, shot, place, owner):
    _, rows, width = slowness.shape
    outs = [(RADIX, rows // (2 * RADIX), width // RADIX)] * RADIX + [(rows, width)]
    got = pl.pallas_call(
        cut_kernel,
        grid_spec=pltpu.PrefetchScalarGridSpec(
            num_scalar_prefetch=4,
            grid=(1,),
            in_specs=[whole(slowness.shape)],
            out_specs=[whole(o) for o in outs],
        ),
        out_shape=[jax.ShapeDtypeStruct(o, F32) for o in outs],
        compiler_params=params(),
        cost_estimate=LONG,
        name="cut_slab",
    )(shift, shot, place, owner, slowness)
    return got[:RADIX], got[RADIX]


def regroup_kernel(*refs):
    ins, outs = refs[:RADIX], refs[-RADIX:]
    for t in range(RADIX):
        for s in range(RADIX):
            outs[t][s] = ins[s][t]


def regroup_stage(pieces, after):
    shape = pieces[0].shape
    return pl.pallas_call(
        regroup_kernel,
        grid=(1,),
        in_specs=[whole(shape)] * RADIX + [ANY],
        out_specs=[whole(shape)] * RADIX,
        out_shape=[jax.ShapeDtypeStruct(shape, F32)] * RADIX,
        compiler_params=params(),
        cost_estimate=LONG,
        name="regroup_slab",
    )(*pieces, after)


def choose_kernel(place_ref, owner_ref, *refs):
    pieces, out_ref = refs[:RADIX], refs[-1]
    at = lax.rem(owner_ref[0] - place_ref[0] + RADIX, RADIX)
    for t, piece in enumerate(pieces):

        @pl.when(at == t)
        def _():
            out_ref[...] = piece[...]


def choose_stage(pieces, place, owner, after):
    shape = pieces[0].shape
    return pl.pallas_call(
        choose_kernel,
        grid_spec=pltpu.PrefetchScalarGridSpec(
            num_scalar_prefetch=2,
            grid=(1,),
            in_specs=[whole(shape)] * RADIX + [ANY] * len(after),
            out_specs=whole(shape),
        ),
        out_shape=jax.ShapeDtypeStruct(shape, F32),
        compiler_params=params(),
        cost_estimate=LONG,
        name="choose_slab",
    )(place, owner, *pieces, *far(after))


def phase_kernel(slot_ref, place_ref, shot_ref, *refs):
    pieces, (cos_ref, sin_ref) = refs[: 2 * RADIX], refs[-2:]
    part = pieces[0].shape[1]
    omega = omega_of(slot_ref[0])
    for n, piece in enumerate(pieces):
        t, other = n % RADIX, n // RADIX
        shot = shot_ref[0] if other == 0 else 1 - shot_ref[0]
        row = 2 * lax.rem(place_ref[0] + t, RADIX) + shot
        at = pl.ds(pl.multiple_of(row * part, part), part)
        for s in range(RADIX):
            theta = omega * (piece[s] - ref_slow) * dz_km
            cos_ref[s, at, :], sin_ref[s, at, :] = phase_parts(theta)


def phase_stage(pieces, slot, place, shot, after):
    _, part, cols = pieces[0].shape
    shape = (RADIX, part * len(pieces), cols)
    return pl.pallas_call(
        phase_kernel,
        grid_spec=pltpu.PrefetchScalarGridSpec(
            num_scalar_prefetch=3,
            grid=(1,),
            in_specs=[whole(p.shape) for p in pieces] + [ANY],
            out_specs=[whole(shape)] * 2,
        ),
        out_shape=[jax.ShapeDtypeStruct(shape, F32)] * 2,
        compiler_params=params(),
        cost_estimate=BRIEF,
        name="phases",
    )(slot, place, shot, *pieces, after)


def image_kernel(chunks, early_ref, *refs):
    out_ref = refs[-1]
    count = (len(refs) - 1) // chunks
    out_ref[0] = early_ref[...]
    part = refs[0].shape[0]
    for c in range(chunks):
        mine = refs[c * count : (c + 1) * count]
        total = mine[0][...]
        for ref in mine[1:]:
            total = total + ref[...]
        out_ref[1, pl.ds(c * part, part), :] = total


def image_stage(early, groups):
    rows, cols = early.shape
    args = [early] + [piece for group in groups for piece in group]
    return pl.pallas_call(
        lambda *refs: image_kernel(len(groups), *refs),
        out_shape=jax.ShapeDtypeStruct((NZ, rows, cols), F32),
        compiler_params=params(),
        cost_estimate=LONG,
        name="image_sum",
    )(*args)


def shifted(value, axis, step):
    count = lax.axis_size(axis)
    return lax.ppermute(value, axis, [((i + step) % count, i) for i in range(count)])


def swap_slots(pieces, axis):
    count = len(pieces)
    sent = [lax.ppermute(pieces[s], axis, [(i, (i + s) % count) for i in range(count)]) for s in range(1, count)]
    return [pieces[0]] + [sent[count - s - 1] for s in range(1, count)]


def swap_pairs(pieces, axis):
    count = len(pieces)
    return [pieces[0]] + [
        lax.ppermute(pieces[s], axis, [(i, i ^ s) for i in range(count)]) for s in range(1, count)
    ]


def gather_slots(piece, axis):
    return [piece] + [shifted(piece, axis, s) for s in range(1, lax.axis_size(axis))]


CHUNKS = 2


def body(source_field, receiver_field, slowness, owner, freq_index):
    rows, width = source_field.shape[2:]
    row_count = lax.axis_size("row")
    freq_count = lax.axis_size("freq")
    row_at = lax.axis_index("row")
    place = lax.axis_index("freq")[None]
    shot = lax.axis_index("shot")[None]
    slot = freq_index
    ringed = row_count == RADIX and freq_count == RADIX and slowness.shape[0] == 1
    ringed = ringed and lax.axis_size("shot") == 2
    shift = row_at[None] if ringed else jnp.zeros((1,), jnp.int32)
    if not ringed:
        return general(source_field, receiver_field, slowness, owner, slot, shift, place)

    turned, late = cut_stage(slowness, shift, shot, place, owner)
    turned = swap_pairs(turned, "row")
    late = lax.psum(late, "freq")
    s_first, blocks = first_stage(source_field, shift, slot, None, 2, (turned[0],))
    s_mid = swap_pairs(s_first, "row")
    r_first, _ = first_stage(receiver_field, shift, slot, blocks, 2, turned[1:])
    r_mid = swap_pairs(r_first, "row")
    shares = swap_slots(regroup_stage(turned, r_first[0]), "freq")
    gathered = gather_slots(choose_stage(shares, place, owner, [s_mid[2], r_mid[2]]), "freq")
    gathered += [lax.ppermute(g, "shot", [(0, 1), (1, 0)]) for g in gathered]
    s_half = half_stage(s_mid, blocks, shift)
    phases = phase_stage(gathered, slot, place, shot, s_half)

    s_pieces, s_held = middle_stage([s_half], phases, blocks, shift, 1, None, r_mid[1:])
    s_last = swap_pairs(s_pieces[0], "row")
    r_pieces, term = middle_stage(r_mid, phases, blocks, shift, CHUNKS, s_held)
    r_last = [swap_pairs(p, "row") for p in r_pieces]
    total = lax.psum_scatter(term, "freq", scatter_dimension=0, tiled=False)
    pairs = []
    for r in range(RADIX):
        for f in range(RADIX):
            pairs.append((r * RADIX + f, (r ^ f) * RADIX + r))
    first_image = lax.ppermute(total, ("row", "freq"), pairs)

    source_out, _ = last_stage(s_last, late, blocks, shift, slot, place, 0, rows, None, None)
    receiver_out, groups = None, []
    for c in range(CHUNKS):
        receiver_out, terms = last_stage(
            r_last[c], late, blocks, shift, slot, place, c * (rows // CHUNKS), rows, source_out, receiver_out
        )
        groups.append(swap_slots(terms, "freq"))
    return (source_out, receiver_out, image_stage(first_image, groups))


def general(source_field, receiver_field, slowness, owner, slot, shift, place):
    rows, width = source_field.shape[2:]
    slab_dev = slowness.shape[0]
    slabs = []
    for depth in range(NZ):
        chosen = owner[depth]
        kept = lax.dynamic_index_in_dim(slowness, chosen % slab_dev, 0, keepdims=False)
        slabs.append(lax.psum(jnp.where(place[0] == chosen // slab_dev, kept, 0.0), "freq"))
    s_first, blocks = first_stage(source_field, shift, slot, None, 1)
    r_first, _ = first_stage(receiver_field, shift, slot, blocks, 1)

    def to_columns(pieces):
        whole_rows = jnp.concatenate(pieces, axis=2)
        return lax.all_to_all(whole_rows, "row", split_axis=2, concat_axis=1, tiled=True)

    def to_rows(pieces):
        whole_cols = jnp.concatenate(pieces, axis=1)
        return lax.all_to_all(whole_cols, "row", split_axis=1, concat_axis=2, tiled=True)

    s_mid = jnp.split(to_columns(s_first), RADIX, axis=1)
    r_mid = jnp.split(to_columns(r_first), RADIX, axis=1)
    turned = lax.all_to_all(slabs[0], "row", split_axis=1, concat_axis=0, tiled=True)
    theta = omega_of(slot[0]) * (turned - ref_slow) * dz_km
    theta = theta.reshape(RADIX, -1, theta.shape[1])
    phases = (jnp.cos(theta), jnp.sin(theta))
    s_pieces, s_held = middle_stage([half_stage(s_mid, blocks, shift)], phases, blocks, shift, 1, None)
    r_pieces, term = middle_stage(r_mid, phases, blocks, shift, 1, s_held)
    s_last = jnp.split(to_rows(s_pieces[0]), RADIX, axis=2)
    r_last = jnp.split(to_rows(r_pieces[0]), RADIX, axis=2)
    source_out, _ = last_stage(s_last, slabs[1], blocks, shift, slot, shift, 0, rows, None, None)
    receiver_out, terms = last_stage(
        r_last, slabs[1], blocks, shift, slot, shift, 0, rows, source_out, None
    )
    term = term.reshape(-1, term.shape[2])
    images = [lax.all_to_all(term, "row", split_axis=0, concat_axis=1, tiled=True)]
    images.append(jnp.concatenate(terms, axis=1))
    parts = [lax.psum_scatter(t, "freq", scatter_dimension=1, tiled=True) for t in images]
    return (source_out, receiver_out, jnp.stack(parts))


def solution(mesh):
    in_specs = (
        P(None, ("shot", "freq"), "row", None),
        P(None, ("shot", "freq"), "row", None),
        P("freq", "row", None),
        P(),
        P(("shot", "freq")),
    )
    out_specs = (
        P(None, ("shot", "freq"), "row", None),
        P(None, ("shot", "freq"), "row", None),
        P("shot", "row", "freq"),
    )
    return jax.shard_map(body, mesh=mesh, in_specs=in_specs, out_specs=out_specs, check_vma=False)
```

```python
import math

import jax
import jax.numpy as jnp
import numpy as np
from jax import lax
from jax.experimental import pallas as pl
from jax.experimental.pallas import tpu as pltpu
from jax.sharding import PartitionSpec as P

NZ = 2

dz_km = 0.01
dx_km = 0.0125
ref_slow = 0.5
base_hertz = 3.0
step_hertz = 4.0
taper = 0.5

RADIX = 4
BRIEF = pl.CostEstimate(flops=1000, bytes_accessed=1000, transcendentals=0)
LONG = pl.CostEstimate(flops=10**11, bytes_accessed=10**7, transcendentals=0)
LIMIT = 20 * 1024 * 1024
F32 = jnp.float32
ANY = pl.BlockSpec(memory_space=pl.ANY)
BF16 = jnp.bfloat16


def params():
    return pltpu.CompilerParams(vmem_limit_bytes=LIMIT)


def whole(shape):
    return pl.BlockSpec(shape, lambda *_: (0,) * len(shape))


def far(arrays):
    return [pltpu.with_memory_space_constraint(a, pltpu.HBM) for a in arrays]


def omega_of(slot):
    return 2.0 * math.pi * (base_hertz + step_hertz * slot.astype(F32))


def add(a, b):
    return (a[0] + b[0], a[1] + b[1])


def sub(a, b):
    return (a[0] - b[0], a[1] - b[1])


def add_i(a, b):
    return (a[0] - b[1], a[1] + b[0])


def sub_i(a, b):
    return (a[0] + b[1], a[1] - b[0])


def spread_blocks(x):
    even, odd = add(x[0], x[2]), add(x[1], x[3])
    plus, minus = sub(x[0], x[2]), sub(x[1], x[3])
    return [add(even, odd), sub_i(plus, minus), sub(even, odd), add_i(plus, minus)]


def join_blocks(y):
    even, odd = add(y[0], y[2]), add(y[1], y[3])
    plus, minus = sub(y[0], y[2]), sub(y[1], y[3])
    return [add(even, odd), add_i(plus, minus), sub(even, odd), sub_i(plus, minus)]


def halves(x):
    high = x.astype(BF16)
    return high, (x - high.astype(F32)).astype(BF16)


def dot(a, b):
    return jnp.dot(a, b, preferred_element_type=F32)


def times_right(x, high, low):
    xr, xi = halves(x[0]), halves(x[1])
    out = []
    for left, right, sign in ((xr, xi, -1), (xi, xr, 1)):
        a = jnp.concatenate([left[0], right[0] * sign], axis=1)
        b = jnp.concatenate([left[1], right[1] * sign], axis=1)
        out.append(dot(a, high) + dot(a, low) + dot(b, high))
    return tuple(out)


def times_left(x, high, low):
    xr, xi = halves(x[0]), halves(x[1])
    size = high.shape[1]
    lead_h = jnp.concatenate([high[:size], high[size:]], axis=1)
    lead_l = jnp.concatenate([low[:size], low[size:]], axis=1)
    out = []
    for left, right, sign in ((xr, xi, -1), (xi, xr, 1)):
        a = jnp.concatenate([left[0], right[0] * sign], axis=0)
        b = jnp.concatenate([left[1], right[1] * sign], axis=0)
        out.append(dot(lead_h, a) + dot(lead_l, a) + dot(lead_h, b))
    return tuple(out)


def block_of(me, slot):
    return lax.bitwise_xor(me, slot)


def convolve(x, high_ref, low_ref, left, me):
    times = times_left if left else times_right
    x = spread_blocks(x)
    flip = lax.bitwise_and(me, 1) * 2
    y = []
    for k in range(RADIX):
        at = k if left else (RADIX - k) % RADIX
        if k % 2 == 1:
            at = lax.bitwise_xor(flip, at)
        y.append(times(x[k], high_ref[at], low_ref[at]))
    return join_blocks(y)


def phase_parts(theta):
    q = theta * theta
    sin_v = theta * (1.0 + q * (-1 / 6 + q * (1 / 120 + q * (-1 / 5040 + q * (1 / 362880)))))
    cos_v = 1.0 + q * (-0.5 + q * (1 / 24 + q * (-1 / 720 + q * (1 / 40320 - q * (1 / 3628800)))))
    return cos_v, sin_v


def rotate(x, cos_v, sin_v):
    return (x[0] * cos_v - x[1] * sin_v, x[1] * cos_v + x[0] * sin_v)


def cosine_table(length):
    k = np.arange(length // 2)[:, None]
    n = np.arange(length)[None, :]
    table = np.cos(2.0 * math.pi * ((k * n) % length) / length) * np.where(k == 0, 1.0, 2.0)
    return jnp.asarray(table / length, F32)


def propagator(omega, m, length):
    ws0 = omega * ref_slow
    wave = m * (2.0 * math.pi / (length * dx_km))
    square = wave * wave
    kmax = math.pi / dx_km
    damp = jnp.exp(-taper * square / (kmax * kmax))
    phase = dz_km * (0.5 * ws0 - 0.5 * square / ws0)
    return damp * jnp.cos(phase), damp * jnp.sin(phase)


def make_blocks(omega, table_ref, high_ref, low_ref):
    half, length = table_ref.shape
    block = length // RADIX
    m = lax.broadcasted_iota(jnp.int32, (8, half), 1).astype(F32)
    g = propagator(omega, m, length)
    g = tuple(jnp.transpose(part) for part in g)
    lane = lax.broadcasted_iota(jnp.int32, (8, length), 1)
    row = lax.broadcasted_iota(jnp.int32, (8, length), 0)
    last = propagator(omega, jnp.full((8, length), half, F32), length)
    flip = jnp.where(lane % 2 == 0, 1.0, -1.0) / length
    flip = jnp.where(row == 0, flip, 0.0)
    total = [part * flip for part in last]
    for j in range(half // 8):
        here = table_ref[pl.ds(8 * j, 8), :]
        for c in range(2):
            total[c] = total[c] + here * g[c][8 * j : 8 * j + 8, 0:1]
    rows = []
    for c in range(2):
        line = jnp.sum(total[c], axis=0, keepdims=True) * (1.0 / RADIX)
        rows.append(
            pltpu.roll(jnp.broadcast_to(line, (block, length)), 0, 1, stride=1, stride_axis=0)
        )
    parts = [tuple(r[:, e * block : (e + 1) * block] for r in rows) for e in range(RADIX)]
    for k, value in enumerate(join_blocks(parts)):
        for c in range(2):
            high, low = halves(value[c])
            high_ref[k, pl.ds(c * block, block), :] = high
            low_ref[k, pl.ds(c * block, block), :] = low


def pick(ref_value, swap):
    return (ref_value[1], ref_value[0]) if swap else (ref_value[0], ref_value[1])


def store(ref, value, swap):
    ref[0], ref[1] = (value[1], value[0]) if swap else (value[0], value[1])


def first_kernel(form, waits, shift_ref, slot_ref, *refs):
    fields, refs = refs[:RADIX], refs[RADIX:]
    if waits:
        refs = refs[waits:]
    if form:
        table_ref, refs = refs[0], refs[1:]
        outs, (high_ref, low_ref) = refs[:RADIX], refs[RADIX:]

        @pl.when(pl.program_id(0) == 0)
        def _():
            make_blocks(omega_of(slot_ref[0]), table_ref, high_ref, low_ref)

    else:
        (high_ref, low_ref), outs = refs[:2], refs[2:]
    x = [pick(f[:, 0], not form) for f in fields]
    for ref, value in zip(outs, convolve(x, high_ref, low_ref, False, shift_ref[0])):
        store(ref, value, False)


def first_stage(field, shift, slot, blocks, steps, after=()):
    _, _, rows, width = field.shape
    block = width // RADIX
    part = rows // steps
    form = blocks is None
    shape = (RADIX, 2 * block, block)
    specs = [
        pl.BlockSpec((2, 1, part, block), lambda i, sh, _, s=s: (0, 0, i, block_of(sh[0], s)))
        for s in range(RADIX)
    ]
    outs = [pltpu.HBM((2, rows, block), F32)] * RADIX
    out_specs = [pl.BlockSpec((2, part, block), lambda i, *_: (0, i, 0))] * RADIX
    if form:
        more = (cosine_table(width),)
        outs = outs + [jax.ShapeDtypeStruct(shape, BF16)] * 2
        out_specs = out_specs + [whole(shape)] * 2
    else:
        more = tuple(blocks)
    got = pl.pallas_call(
        lambda *refs: first_kernel(form, len(after), *refs),
        grid_spec=pltpu.PrefetchScalarGridSpec(
            num_scalar_prefetch=2,
            grid=(steps,),
            in_specs=specs + [ANY] * len(after) + [whole(a.shape) for a in more],
            out_specs=out_specs,
        ),
        out_shape=outs,
        compiler_params=params(),
        cost_estimate=LONG,
        name="along_y_first_s" if form else "along_y_first_r",
    )(shift, slot, *[field] * RADIX, *far(after), *more)
    return (got[:RADIX], tuple(got[RADIX:])) if form else (got, blocks)


def half_kernel(shift_ref, *refs):
    fields, (high_ref, low_ref, out_ref) = refs[:RADIX], refs[RADIX:]
    x = convolve([pick(f, False) for f in fields], high_ref, low_ref, True, shift_ref[0])
    for s in range(RADIX):
        store(out_ref.at[s], x[s], False)


def half_stage(fields, blocks, shift):
    _, rows, cols = fields[0].shape
    args = list(fields) + list(blocks)
    shape = (RADIX, 2, rows, cols)
    return pl.pallas_call(
        half_kernel,
        grid_spec=pltpu.PrefetchScalarGridSpec(
            num_scalar_prefetch=1,
            grid=(1,),
            in_specs=[whole(a.shape) for a in args],
            out_specs=whole(shape),
        ),
        out_shape=jax.ShapeDtypeStruct(shape, F32),
        compiler_params=params(),
        cost_estimate=LONG,
        name="along_x_s_first",
    )(shift, *far(fields), *blocks)


def middle_kernel(count, with_image, waits, shift_ref, place_ref, *refs):
    if with_image:
        fields, refs = refs[:RADIX], refs[RADIX:]
        other_ref, refs = refs[0], refs[1:]
    else:
        half_ref, refs = refs[0], refs[1:]
    cos_ref, sin_ref, high_ref, low_ref = refs[:4]
    refs = refs[4 + waits :]
    outs, extra = refs[: RADIX * count], refs[RADIX * count :]
    if with_image:
        x = convolve([pick(f, False) for f in fields], high_ref, low_ref, True, shift_ref[0])
    else:
        x = [pick(half_ref.at[s], False) for s in range(RADIX)]
    x = [rotate(x[s], cos_ref[s], sin_ref[s]) for s in range(RADIX)]
    for s in range(RADIX):
        if with_image:
            extra[2][s] = other_ref[s, 0] * x[s][1] + other_ref[s, 1] * x[s][0]
        else:
            store(extra[0].at[s], x[s], False)
    if with_image:
        mine = lax.bitwise_and(place_ref[0], 1)
        for j in range(RADIX // 2):
            extra[0][j] = extra[2][mine + 2 * j]
            extra[1][j] = extra[2][1 - mine + 2 * j]
    x = convolve(x, high_ref, low_ref, True, shift_ref[0])
    part = x[0][0].shape[0] // count
    for s in range(RADIX):
        for c in range(count):
            value = tuple(v[c * part : (c + 1) * part] for v in x[s])
            store(outs[s * count + c], value, False)


def middle_stage(fields, phases, blocks, shift, place, count, other, after=()):
    with_image = other is not None
    _, rows, cols = phases[0].shape
    piece = pltpu.HBM((2, rows // count, cols), F32)
    fields = far(fields) if with_image else fields
    extra = [(RADIX // 2, rows, cols)] * 2 if with_image else [(RADIX, 2, rows, cols)]
    args = list(fields) + ([other] if with_image else []) + list(phases) + list(blocks)
    outs = [piece] * (RADIX * count) + [jax.ShapeDtypeStruct(e, F32) for e in extra]
    got = pl.pallas_call(
        lambda *refs: middle_kernel(count, with_image, len(after), *refs),
        grid_spec=pltpu.PrefetchScalarGridSpec(
            num_scalar_prefetch=2,
            grid=(1,),
            in_specs=[whole(a.shape) for a in args] + [ANY] * len(after),
            out_specs=[whole(o.shape) for o in outs],
            scratch_shapes=[pltpu.VMEM((RADIX, rows, cols), F32)] if with_image else [],
        ),
        out_shape=outs,
        compiler_params=params(),
        cost_estimate=LONG,
        name="along_x_r" if with_image else "along_x_s_second",
    )(shift, place, *args, *far(after))
    pieces = [[got[s * count + c] for s in range(RADIX)] for c in range(count)]
    return pieces, got[RADIX * count :] if with_image else got[-1]


def last_kernel(with_image, shift_ref, slot_ref, place_ref, *refs):
    fields, refs = refs[:RADIX], refs[RADIX:]
    slab_ref, high_ref, low_ref = refs[:3]
    refs = refs[3:]
    if with_image:
        other_ref = refs[0]
        out_ref, terms, line = refs[-(RADIX + 2)], refs[-(RADIX + 1) : -1], refs[-1]
    else:
        out_ref = refs[-1]
    block = fields[0].shape[2]
    omega = omega_of(slot_ref[0])
    x = convolve([pick(f, False) for f in fields], high_ref, low_ref, False, shift_ref[0])
    for s in range(RADIX):
        at = pl.ds(pl.multiple_of(block_of(shift_ref[0], s) * block, block), block)
        theta = omega * (slab_ref[:, at] - ref_slow) * dz_km
        value = rotate(x[s], *phase_parts(theta))
        if with_image:
            line[:, at] = other_ref[0, 0, :, at] * value[1] + other_ref[1, 0, :, at] * value[0]
            value = (value[1], value[0])
        out_ref[0, 0, :, at] = value[0]
        out_ref[1, 0, :, at] = value[1]
    if with_image:
        count = len(terms)
        part = line.shape[1] // count
        for t in range(count):
            at = pl.ds(pl.multiple_of(lax.rem(place_ref[0] + t, count) * part, part), part)
            terms[t][...] = line[:, at]


def last_stage(fields, slab, blocks, shift, slot, place, start, rows, other, held, after=()):
    _, part, block = fields[0].shape
    width = block * RADIX
    with_image = other is not None
    row = start // part
    wide = pl.BlockSpec((2, 1, part, width), lambda i, *_: (0, 0, row, 0))
    args = far(fields) + [slab] + list(blocks)
    specs = [whole(f.shape) for f in fields]
    specs += [pl.BlockSpec((part, width), lambda i, *_: (row, 0))]
    specs += [whole(b.shape) for b in blocks]
    outs = [jax.ShapeDtypeStruct((2, 1, rows, width), F32)]
    out_specs = [wide]
    scratch = []
    if with_image:
        args += far([other])
        specs.append(wide)
        cols = width // RADIX
        outs += [jax.ShapeDtypeStruct((part, cols), F32)] * RADIX
        out_specs += [whole((part, cols))] * RADIX
        scratch = [pltpu.VMEM((part, width), F32)]
    alias = {}
    if held is not None:
        alias = {3 + len(args): 0}
        args += far([held])
        specs.append(ANY)
    args += far(after)
    specs += [ANY] * len(after)
    got = pl.pallas_call(
        lambda *refs: last_kernel(with_image, *refs),
        grid_spec=pltpu.PrefetchScalarGridSpec(
            num_scalar_prefetch=3,
            grid=(1,),
            in_specs=specs,
            out_specs=out_specs,
            scratch_shapes=scratch,
        ),
        out_shape=outs,
        input_output_aliases=alias,
        compiler_params=params(),
        cost_estimate=LONG,
        name="along_y_last_r" if with_image else "along_y_last_s",
    )(shift, slot, place, *args)
    return got[0], got[1:]


def cut_kernel(shift_ref, shot_ref, place_ref, owner_ref, slab_ref, *outs):
    part, block = outs[0].shape[1:]
    for t in range(RADIX):
        row = 2 * lax.rem(place_ref[0] + t, RADIX) + shot_ref[0]
        rows = pl.ds(pl.multiple_of(row * part, part), part)
        for s in range(RADIX):
            cols = pl.ds(pl.multiple_of(block_of(shift_ref[0], s) * block, block), block)
            outs[s][t] = slab_ref[0, rows, cols]
    kept = (owner_ref[NZ - 1] == place_ref[0]).astype(F32)
    half = outs[-1].shape[0]
    outs[-1][...] = slab_ref[0, pl.ds(pl.multiple_of(shot_ref[0] * half, half), half), :] * kept


def cut_stage(slowness, shift, shot, place, owner):
    _, rows, width = slowness.shape
    outs = [(RADIX, rows // (2 * RADIX), width // RADIX)] * RADIX + [(rows // 2, width)]
    got = pl.pallas_call(
        cut_kernel,
        grid_spec=pltpu.PrefetchScalarGridSpec(
            num_scalar_prefetch=4,
            grid=(1,),
            in_specs=[whole(slowness.shape)],
            out_specs=[whole(o) for o in outs],
        ),
        out_shape=[jax.ShapeDtypeStruct(o, F32) for o in outs],
        compiler_params=params(),
        cost_estimate=LONG,
        name="cut_slab",
    )(shift, shot, place, owner, slowness)
    return got[:RADIX], got[RADIX]


def regroup_kernel(*refs):
    ins, outs = refs[:RADIX], refs[-RADIX:]
    for t in range(RADIX):
        for s in range(RADIX):
            outs[t][s] = ins[s][t]


def regroup_stage(pieces, after):
    shape = pieces[0].shape
    return pl.pallas_call(
        regroup_kernel,
        grid=(1,),
        in_specs=[whole(shape)] * RADIX + [ANY],
        out_specs=[whole(shape)] * RADIX,
        out_shape=[jax.ShapeDtypeStruct(shape, F32)] * RADIX,
        compiler_params=params(),
        cost_estimate=LONG,
        name="regroup_slab",
    )(*far(pieces), after)


def choose_kernel(place_ref, owner_ref, *refs):
    pieces, out_ref = refs[:RADIX], refs[-1]
    at = lax.rem(owner_ref[0] - place_ref[0] + RADIX, RADIX)
    for t, piece in enumerate(pieces):

        @pl.when(at == t)
        def _():
            out_ref[...] = piece[...]


def choose_stage(pieces, place, owner, after):
    shape = pieces[0].shape
    return pl.pallas_call(
        choose_kernel,
        grid_spec=pltpu.PrefetchScalarGridSpec(
            num_scalar_prefetch=2,
            grid=(1,),
            in_specs=[whole(shape)] * RADIX + [ANY] * len(after),
            out_specs=whole(shape),
        ),
        out_shape=jax.ShapeDtypeStruct(shape, F32),
        compiler_params=params(),
        cost_estimate=LONG,
        name="choose_slab",
    )(place, owner, *pieces, *far(after))


def phase_kernel(slot_ref, place_ref, shot_ref, *refs):
    pieces, (cos_ref, sin_ref) = refs[: 2 * RADIX], refs[-2:]
    part = pieces[0].shape[1]
    omega = omega_of(slot_ref[0])
    for n, piece in enumerate(pieces):
        t, other = n % RADIX, n // RADIX
        shot = shot_ref[0] if other == 0 else 1 - shot_ref[0]
        row = 2 * lax.rem(place_ref[0] + t, RADIX) + shot
        at = pl.ds(pl.multiple_of(row * part, part), part)
        for s in range(RADIX):
            theta = omega * (piece[s] - ref_slow) * dz_km
            cos_ref[s, at, :], sin_ref[s, at, :] = phase_parts(theta)


def phase_stage(pieces, slot, place, shot, after):
    _, part, cols = pieces[0].shape
    shape = (RADIX, part * len(pieces), cols)
    return pl.pallas_call(
        phase_kernel,
        grid_spec=pltpu.PrefetchScalarGridSpec(
            num_scalar_prefetch=3,
            grid=(1,),
            in_specs=[whole(p.shape) for p in pieces] + [ANY],
            out_specs=[whole(shape)] * 2,
        ),
        out_shape=[jax.ShapeDtypeStruct(shape, F32)] * 2,
        compiler_params=params(),
        cost_estimate=BRIEF,
        name="phases",
    )(slot, place, shot, *pieces, after)


def add_kernel(a_ref, b_ref, *refs):
    refs[-1][...] = a_ref[...] + b_ref[...]


def add_stage(a, b, name, after=()):
    return pl.pallas_call(
        add_kernel,
        grid=(1,),
        in_specs=[whole(a.shape)] * 2 + [ANY] * len(after),
        out_specs=whole(a.shape),
        out_shape=jax.ShapeDtypeStruct(a.shape, F32),
        compiler_params=params(),
        cost_estimate=BRIEF,
        name=name,
    )(a, b, *far(after))


def fold_kernel(place_ref, a_ref, b_ref, keep_ref, send_ref):
    mine = lax.shift_right_logical(place_ref[0], 1)
    keep_ref[...] = a_ref[mine] + b_ref[mine]
    send_ref[...] = a_ref[1 - mine] + b_ref[1 - mine]


def fold_stage(a, b, place):
    shape = a.shape[1:]
    return pl.pallas_call(
        fold_kernel,
        grid_spec=pltpu.PrefetchScalarGridSpec(
            num_scalar_prefetch=1,
            grid=(1,),
            in_specs=[whole(a.shape)] * 2,
            out_specs=[whole(shape)] * 2,
        ),
        out_shape=[jax.ShapeDtypeStruct(shape, F32)] * 2,
        compiler_params=params(),
        cost_estimate=BRIEF,
        name="first_image_fold",
    )(place, a, b)


def join_kernel(shot_ref, a_ref, b_ref, out_ref):
    half = a_ref.shape[0]
    out_ref[pl.ds(pl.multiple_of(shot_ref[0] * half, half), half), :] = a_ref[...]
    out_ref[pl.ds(pl.multiple_of((1 - shot_ref[0]) * half, half), half), :] = b_ref[...]


def join_stage(a, b, shot):
    shape = (2 * a.shape[0], a.shape[1])
    return pl.pallas_call(
        join_kernel,
        grid_spec=pltpu.PrefetchScalarGridSpec(
            num_scalar_prefetch=1,
            grid=(1,),
            in_specs=[whole(a.shape)] * 2,
            out_specs=whole(shape),
        ),
        out_shape=jax.ShapeDtypeStruct(shape, F32),
        compiler_params=params(),
        cost_estimate=BRIEF,
        name="late_join",
    )(shot, a, b)


def image_kernel(chunks, early_ref, *refs):
    out_ref = refs[-1]
    count = (len(refs) - 1) // chunks
    out_ref[0] = early_ref[...]
    part = refs[0].shape[0]
    for c in range(chunks):
        mine = refs[c * count : (c + 1) * count]
        total = mine[0][...]
        for ref in mine[1:]:
            total = total + ref[...]
        out_ref[1, pl.ds(c * part, part), :] = total


def image_stage(early, groups):
    rows, cols = early.shape
    args = [early] + [piece for group in groups for piece in group]
    return pl.pallas_call(
        lambda *refs: image_kernel(len(groups), *refs),
        out_shape=jax.ShapeDtypeStruct((NZ, rows, cols), F32),
        compiler_params=params(),
        cost_estimate=LONG,
        name="image_sum",
    )(*args)


def shifted(value, axis, step):
    count = lax.axis_size(axis)
    return lax.ppermute(value, axis, [((i + step) % count, i) for i in range(count)])


def swap_slots(pieces, axis):
    count = len(pieces)
    sent = [lax.ppermute(pieces[s], axis, [(i, (i + s) % count) for i in range(count)]) for s in range(1, count)]
    return [pieces[0]] + [sent[count - s - 1] for s in range(1, count)]


def paired(value, axis, bits):
    return lax.ppermute(value, axis, [(i, i ^ bits) for i in range(lax.axis_size(axis))])


def swap_pairs(pieces, axis):
    count = len(pieces)
    return [pieces[0]] + [
        lax.ppermute(pieces[s], axis, [(i, i ^ s) for i in range(count)]) for s in range(1, count)
    ]


def gather_slots(piece, axis):
    return [piece] + [shifted(piece, axis, s) for s in range(1, lax.axis_size(axis))]


CHUNKS = 2


def body(source_field, receiver_field, slowness, owner, freq_index):
    rows, width = source_field.shape[2:]
    row_count = lax.axis_size("row")
    freq_count = lax.axis_size("freq")
    row_at = lax.axis_index("row")
    place = lax.axis_index("freq")[None]
    shot = lax.axis_index("shot")[None]
    slot = freq_index
    ringed = row_count == RADIX and freq_count == RADIX and slowness.shape[0] == 1
    ringed = ringed and lax.axis_size("shot") == 2
    shift = row_at[None] if ringed else jnp.zeros((1,), jnp.int32)
    if not ringed:
        return general(source_field, receiver_field, slowness, owner, slot, shift, place)

    turned, late = cut_stage(slowness, shift, shot, place, owner)
    turned = swap_pairs(turned, "row")
    late = add_stage(late, paired(late, "freq", 2), "late_first")
    s_first, blocks = first_stage(source_field, shift, slot, None, 2, (turned[0],))
    s_mid = swap_pairs(s_first, "row")
    r_first, _ = first_stage(receiver_field, shift, slot, blocks, 2, turned[1:])
    r_mid = swap_pairs(r_first, "row")
    shares = swap_slots(regroup_stage(turned, r_first[0]), "freq")
    gathered = gather_slots(choose_stage(shares, place, owner, [s_mid[2], r_mid[2], late]), "freq")
    gathered += [lax.ppermute(g, "shot", [(0, 1), (1, 0)]) for g in gathered]
    s_half = half_stage(s_mid, blocks, shift)
    phases = phase_stage(gathered, slot, place, shot, s_half)

    s_pieces, s_held = middle_stage([s_half], phases, blocks, shift, place, 1, None, r_mid[1:])
    s_last = swap_pairs(s_pieces[0], "row")
    late_total = add_stage(late, paired(late, "freq", 1), "late_second")
    r_pieces, term = middle_stage(r_mid, phases, blocks, shift, place, CHUNKS, s_held)
    r_last = [swap_pairs(p, "row") for p in r_pieces]
    late = join_stage(late_total, paired(late_total, "shot", 1), shot)
    keep, send = fold_stage(term[0], paired(term[1], "freq", 1), place)
    total = add_stage(keep, paired(send, "freq", 2), "first_image")
    pairs = []
    for r in range(RADIX):
        for f in range(RADIX):
            pairs.append((r * RADIX + f, (r ^ f) * RADIX + r))

    source_out, _ = last_stage(s_last, late, blocks, shift, slot, place, 0, rows, None, None)
    receiver_out, groups = None, []
    for c in range(CHUNKS):
        receiver_out, terms = last_stage(
            r_last[c], late, blocks, shift, slot, place, c * (rows // CHUNKS), rows, source_out, receiver_out,
            [total] if c == CHUNKS - 1 else [],
        )
        groups.append(swap_slots(terms, "freq"))
    first_image = lax.ppermute(total, ("row", "freq"), pairs)
    return (source_out, receiver_out, image_stage(first_image, groups))


def general(source_field, receiver_field, slowness, owner, slot, shift, place):
    rows, width = source_field.shape[2:]
    slab_dev = slowness.shape[0]
    slabs = []
    for depth in range(NZ):
        chosen = owner[depth]
        kept = lax.dynamic_index_in_dim(slowness, chosen % slab_dev, 0, keepdims=False)
        slabs.append(lax.psum(jnp.where(place[0] == chosen // slab_dev, kept, 0.0), "freq"))
    s_first, blocks = first_stage(source_field, shift, slot, None, 1)
    r_first, _ = first_stage(receiver_field, shift, slot, blocks, 1)

    def to_columns(pieces):
        whole_rows = jnp.concatenate(pieces, axis=2)
        return lax.all_to_all(whole_rows, "row", split_axis=2, concat_axis=1, tiled=True)

    def to_rows(pieces):
        whole_cols = jnp.concatenate(pieces, axis=1)
        return lax.all_to_all(whole_cols, "row", split_axis=1, concat_axis=2, tiled=True)

    s_mid = jnp.split(to_columns(s_first), RADIX, axis=1)
    r_mid = jnp.split(to_columns(r_first), RADIX, axis=1)
    turned = lax.all_to_all(slabs[0], "row", split_axis=1, concat_axis=0, tiled=True)
    theta = omega_of(slot[0]) * (turned - ref_slow) * dz_km
    theta = theta.reshape(RADIX, -1, theta.shape[1])
    phases = (jnp.cos(theta), jnp.sin(theta))
    s_pieces, s_held = middle_stage([half_stage(s_mid, blocks, shift)], phases, blocks, shift, shift, 1, None)
    r_pieces, term = middle_stage(r_mid, phases, blocks, shift, shift, 1, s_held)
    s_last = jnp.split(to_rows(s_pieces[0]), RADIX, axis=2)
    r_last = jnp.split(to_rows(r_pieces[0]), RADIX, axis=2)
    source_out, _ = last_stage(s_last, slabs[1], blocks, shift, slot, shift, 0, rows, None, None)
    receiver_out, terms = last_stage(
        r_last, slabs[1], blocks, shift, slot, shift, 0, rows, source_out, None
    )
    term = jnp.stack([term[0][0], term[1][0], term[0][1], term[1][1]]).reshape(-1, term[0].shape[2])
    images = [lax.all_to_all(term, "row", split_axis=0, concat_axis=1, tiled=True)]
    images.append(jnp.concatenate(terms, axis=1))
    parts = [lax.psum_scatter(t, "freq", scatter_dimension=1, tiled=True) for t in images]
    return (source_out, receiver_out, jnp.stack(parts))


def solution(mesh):
    in_specs = (
        P(None, ("shot", "freq"), "row", None),
        P(None, ("shot", "freq"), "row", None),
        P("freq", "row", None),
        P(),
        P(("shot", "freq")),
    )
    out_specs = (
        P(None, ("shot", "freq"), "row", None),
        P(None, ("shot", "freq"), "row", None),
        P("shot", "row", "freq"),
    )
    return jax.shard_map(body, mesh=mesh, in_specs=in_specs, out_specs=out_specs, check_vma=False)
```

```python
import math

import jax
import jax.numpy as jnp
import numpy as np
from jax import lax
from jax.experimental import pallas as pl
from jax.experimental.pallas import tpu as pltpu
from jax.sharding import PartitionSpec as P

NZ = 2

dz_km = 0.01
dx_km = 0.0125
ref_slow = 0.5
base_hertz = 3.0
step_hertz = 4.0
taper = 0.5

RADIX = 4
BRIEF = pl.CostEstimate(flops=1000, bytes_accessed=1000, transcendentals=0)
LONG = pl.CostEstimate(flops=10**11, bytes_accessed=10**7, transcendentals=0)
LIMIT = 20 * 1024 * 1024
F32 = jnp.float32
ANY = pl.BlockSpec(memory_space=pl.ANY)
BF16 = jnp.bfloat16


def params():
    return pltpu.CompilerParams(vmem_limit_bytes=LIMIT)


def whole(shape):
    return pl.BlockSpec(shape, lambda *_: (0,) * len(shape))


def far(arrays):
    return [pltpu.with_memory_space_constraint(a, pltpu.HBM) for a in arrays]


def omega_of(slot):
    return 2.0 * math.pi * (base_hertz + step_hertz * slot.astype(F32))


def add(a, b):
    return (a[0] + b[0], a[1] + b[1])


def sub(a, b):
    return (a[0] - b[0], a[1] - b[1])


def add_i(a, b):
    return (a[0] - b[1], a[1] + b[0])


def sub_i(a, b):
    return (a[0] + b[1], a[1] - b[0])


def spread_blocks(x):
    even, odd = add(x[0], x[2]), add(x[1], x[3])
    plus, minus = sub(x[0], x[2]), sub(x[1], x[3])
    return [add(even, odd), sub_i(plus, minus), sub(even, odd), add_i(plus, minus)]


def join_blocks(y):
    even, odd = add(y[0], y[2]), add(y[1], y[3])
    plus, minus = sub(y[0], y[2]), sub(y[1], y[3])
    return [add(even, odd), add_i(plus, minus), sub(even, odd), sub_i(plus, minus)]


def halves(x):
    high = x.astype(BF16)
    return high, (x - high.astype(F32)).astype(BF16)


def dot(a, b):
    return jnp.dot(a, b, preferred_element_type=F32)


def times_right(x, high, low):
    xr, xi = halves(x[0]), halves(x[1])
    out = []
    for left, right, sign in ((xr, xi, -1), (xi, xr, 1)):
        a = jnp.concatenate([left[0], right[0] * sign], axis=1)
        b = jnp.concatenate([left[1], right[1] * sign], axis=1)
        out.append(dot(a, high) + dot(a, low) + dot(b, high))
    return tuple(out)


def times_left(x, high, low):
    xr, xi = halves(x[0]), halves(x[1])
    size = high.shape[1]
    lead_h = jnp.concatenate([high[:size], high[size:]], axis=1)
    lead_l = jnp.concatenate([low[:size], low[size:]], axis=1)
    out = []
    for left, right, sign in ((xr, xi, -1), (xi, xr, 1)):
        a = jnp.concatenate([left[0], right[0] * sign], axis=0)
        b = jnp.concatenate([left[1], right[1] * sign], axis=0)
        out.append(dot(lead_h, a) + dot(lead_l, a) + dot(lead_h, b))
    return tuple(out)


def block_of(me, slot):
    return lax.bitwise_xor(me, slot)


def convolve(x, high_ref, low_ref, left, me):
    times = times_left if left else times_right
    x = spread_blocks(x)
    flip = lax.bitwise_and(me, 1) * 2
    y = []
    for k in range(RADIX):
        at = k if left else (RADIX - k) % RADIX
        if k % 2 == 1:
            at = lax.bitwise_xor(flip, at)
        y.append(times(x[k], high_ref[at], low_ref[at]))
    return join_blocks(y)


def phase_parts(theta):
    q = theta * theta
    sin_v = theta * (1.0 + q * (-1 / 6 + q * (1 / 120 + q * (-1 / 5040 + q * (1 / 362880)))))
    cos_v = 1.0 + q * (-0.5 + q * (1 / 24 + q * (-1 / 720 + q * (1 / 40320 - q * (1 / 3628800)))))
    return cos_v, sin_v


def rotate(x, cos_v, sin_v):
    return (x[0] * cos_v - x[1] * sin_v, x[1] * cos_v + x[0] * sin_v)


def cosine_table(length):
    k = np.arange(length // 2)[:, None]
    n = np.arange(length)[None, :]
    table = np.cos(2.0 * math.pi * ((k * n) % length) / length) * np.where(k == 0, 1.0, 2.0)
    return jnp.asarray(table / length, F32)


def propagator(omega, m, length):
    ws0 = omega * ref_slow
    wave = m * (2.0 * math.pi / (length * dx_km))
    square = wave * wave
    kmax = math.pi / dx_km
    damp = jnp.exp(-taper * square / (kmax * kmax))
    phase = dz_km * (0.5 * ws0 - 0.5 * square / ws0)
    return damp * jnp.cos(phase), damp * jnp.sin(phase)


def make_blocks(omega, table_ref, high_ref, low_ref):
    half, length = table_ref.shape
    block = length // RADIX
    m = lax.broadcasted_iota(jnp.int32, (8, half), 1).astype(F32)
    g = propagator(omega, m, length)
    g = tuple(jnp.transpose(part) for part in g)
    lane = lax.broadcasted_iota(jnp.int32, (8, length), 1)
    row = lax.broadcasted_iota(jnp.int32, (8, length), 0)
    last = propagator(omega, jnp.full((8, length), half, F32), length)
    flip = jnp.where(lane % 2 == 0, 1.0, -1.0) / length
    flip = jnp.where(row == 0, flip, 0.0)
    total = [part * flip for part in last]
    for j in range(half // 8):
        here = table_ref[pl.ds(8 * j, 8), :]
        for c in range(2):
            total[c] = total[c] + here * g[c][8 * j : 8 * j + 8, 0:1]
    rows = []
    for c in range(2):
        line = jnp.sum(total[c], axis=0, keepdims=True) * (1.0 / RADIX)
        rows.append(
            pltpu.roll(jnp.broadcast_to(line, (block, length)), 0, 1, stride=1, stride_axis=0)
        )
    parts = [tuple(r[:, e * block : (e + 1) * block] for r in rows) for e in range(RADIX)]
    for k, value in enumerate(join_blocks(parts)):
        for c in range(2):
            high, low = halves(value[c])
            high_ref[k, pl.ds(c * block, block), :] = high
            low_ref[k, pl.ds(c * block, block), :] = low


def pick(ref_value, swap):
    return (ref_value[1], ref_value[0]) if swap else (ref_value[0], ref_value[1])


def store(ref, value, swap):
    ref[0], ref[1] = (value[1], value[0]) if swap else (value[0], value[1])


def first_kernel(form, waits, shift_ref, slot_ref, *refs):
    fields, refs = refs[:RADIX], refs[RADIX:]
    if waits:
        refs = refs[waits:]
    if form:
        table_ref, refs = refs[0], refs[1:]
        outs, (high_ref, low_ref) = refs[:RADIX], refs[RADIX:]

        @pl.when(pl.program_id(0) == 0)
        def _():
            make_blocks(omega_of(slot_ref[0]), table_ref, high_ref, low_ref)

    else:
        (high_ref, low_ref), outs = refs[:2], refs[2:]
    x = [pick(f[:, 0], not form) for f in fields]
    for ref, value in zip(outs, convolve(x, high_ref, low_ref, False, shift_ref[0])):
        store(ref, value, False)


def first_stage(field, shift, slot, blocks, steps, after=()):
    _, _, rows, width = field.shape
    block = width // RADIX
    part = rows // steps
    form = blocks is None
    shape = (RADIX, 2 * block, block)
    specs = [
        pl.BlockSpec((2, 1, part, block), lambda i, sh, _, s=s: (0, 0, i, block_of(sh[0], s)))
        for s in range(RADIX)
    ]
    outs = [pltpu.HBM((2, rows, block), F32)] * RADIX
    out_specs = [pl.BlockSpec((2, part, block), lambda i, *_: (0, i, 0))] * RADIX
    if form:
        more = (cosine_table(width),)
        outs = outs + [jax.ShapeDtypeStruct(shape, BF16)] * 2
        out_specs = out_specs + [whole(shape)] * 2
    else:
        more = tuple(blocks)
    got = pl.pallas_call(
        lambda *refs: first_kernel(form, len(after), *refs),
        grid_spec=pltpu.PrefetchScalarGridSpec(
            num_scalar_prefetch=2,
            grid=(steps,),
            in_specs=specs + [ANY] * len(after) + [whole(a.shape) for a in more],
            out_specs=out_specs,
        ),
        out_shape=outs,
        compiler_params=params(),
        cost_estimate=LONG,
        name="along_y_first_s" if form else "along_y_first_r",
    )(shift, slot, *[field] * RADIX, *far(after), *more)
    return (got[:RADIX], tuple(got[RADIX:])) if form else (got, blocks)


def half_kernel(shift_ref, *refs):
    fields, (high_ref, low_ref, out_ref) = refs[:RADIX], refs[RADIX:]
    x = convolve([pick(f, False) for f in fields], high_ref, low_ref, True, shift_ref[0])
    for s in range(RADIX):
        store(out_ref.at[s], x[s], False)


def half_stage(fields, blocks, shift):
    _, rows, cols = fields[0].shape
    args = list(fields) + list(blocks)
    shape = (RADIX, 2, rows, cols)
    return pl.pallas_call(
        half_kernel,
        grid_spec=pltpu.PrefetchScalarGridSpec(
            num_scalar_prefetch=1,
            grid=(1,),
            in_specs=[whole(a.shape) for a in args],
            out_specs=whole(shape),
        ),
        out_shape=jax.ShapeDtypeStruct(shape, F32),
        compiler_params=params(),
        cost_estimate=LONG,
        name="along_x_s_first",
    )(shift, *far(fields), *blocks)


def middle_kernel(count, with_image, waits, shift_ref, place_ref, *refs):
    if with_image:
        fields, refs = refs[:RADIX], refs[RADIX:]
        other_ref, refs = refs[0], refs[1:]
    else:
        half_ref, refs = refs[0], refs[1:]
    cos_ref, sin_ref, high_ref, low_ref = refs[:4]
    refs = refs[4 + waits :]
    outs, extra = refs[: RADIX * count], refs[RADIX * count :]
    if with_image:
        x = convolve([pick(f, False) for f in fields], high_ref, low_ref, True, shift_ref[0])
    else:
        x = [pick(half_ref.at[s], False) for s in range(RADIX)]
    x = [rotate(x[s], cos_ref[s], sin_ref[s]) for s in range(RADIX)]
    for s in range(RADIX):
        if with_image:
            extra[2][s] = other_ref[s, 0] * x[s][1] + other_ref[s, 1] * x[s][0]
        else:
            store(extra[0].at[s], x[s], False)
    if with_image:
        mine = lax.bitwise_and(place_ref[0], 1)
        for j in range(RADIX // 2):
            extra[0][j] = extra[2][mine + 2 * j]
            extra[1][j] = extra[2][1 - mine + 2 * j]
    x = convolve(x, high_ref, low_ref, True, shift_ref[0])
    part = x[0][0].shape[0] // count
    for s in range(RADIX):
        for c in range(count):
            value = tuple(v[c * part : (c + 1) * part] for v in x[s])
            store(outs[s * count + c], value, False)


def middle_stage(fields, phases, blocks, shift, place, count, other, after=()):
    with_image = other is not None
    _, rows, cols = phases[0].shape
    piece = pltpu.HBM((2, rows // count, cols), F32)
    fields = far(fields) if with_image else fields
    extra = [(RADIX // 2, rows, cols)] * 2 if with_image else [(RADIX, 2, rows, cols)]
    args = list(fields) + ([other] if with_image else []) + list(phases) + list(blocks)
    outs = [piece] * (RADIX * count) + [jax.ShapeDtypeStruct(e, F32) for e in extra]
    got = pl.pallas_call(
        lambda *refs: middle_kernel(count, with_image, len(after), *refs),
        grid_spec=pltpu.PrefetchScalarGridSpec(
            num_scalar_prefetch=2,
            grid=(1,),
            in_specs=[whole(a.shape) for a in args] + [ANY] * len(after),
            out_specs=[whole(o.shape) for o in outs],
            scratch_shapes=[pltpu.VMEM((RADIX, rows, cols), F32)] if with_image else [],
        ),
        out_shape=outs,
        compiler_params=params(),
        cost_estimate=LONG,
        name="along_x_r" if with_image else "along_x_s_second",
    )(shift, place, *args, *far(after))
    pieces = [[got[s * count + c] for s in range(RADIX)] for c in range(count)]
    return pieces, got[RADIX * count :] if with_image else got[-1]


def last_kernel(with_image, shift_ref, slot_ref, place_ref, *refs):
    fields, refs = refs[:RADIX], refs[RADIX:]
    slab_ref, high_ref, low_ref = refs[:3]
    refs = refs[3:]
    if with_image:
        other_ref = refs[0]
        out_ref, keep_ref, send_ref, line = refs[-4:]
    else:
        out_ref = refs[-1]
    block = fields[0].shape[2]
    omega = omega_of(slot_ref[0])
    x = convolve([pick(f, False) for f in fields], high_ref, low_ref, False, shift_ref[0])
    for s in range(RADIX):
        at = pl.ds(pl.multiple_of(block_of(shift_ref[0], s) * block, block), block)
        theta = omega * (slab_ref[:, at] - ref_slow) * dz_km
        value = rotate(x[s], *phase_parts(theta))
        if with_image:
            line[:, at] = other_ref[0, 0, :, at] * value[1] + other_ref[1, 0, :, at] * value[0]
            value = (value[1], value[0])
        out_ref[0, 0, :, at] = value[0]
        out_ref[1, 0, :, at] = value[1]
    if with_image:
        mine = lax.bitwise_and(place_ref[0], 1)
        for j in range(RADIX // 2):
            for ref, first in ((keep_ref, mine), (send_ref, 1 - mine)):
                ref[j] = line[:, pl.ds(pl.multiple_of((first + 2 * j) * block, block), block)]


def last_stage(fields, slab, blocks, shift, slot, place, start, rows, other, held, after=()):
    _, part, block = fields[0].shape
    width = block * RADIX
    with_image = other is not None
    row = start // part
    wide = pl.BlockSpec((2, 1, part, width), lambda i, *_: (0, 0, row, 0))
    args = far(fields) + [slab] + list(blocks)
    specs = [whole(f.shape) for f in fields]
    specs += [pl.BlockSpec((part, width), lambda i, *_: (row, 0))]
    specs += [whole(b.shape) for b in blocks]
    outs = [jax.ShapeDtypeStruct((2, 1, rows, width), F32)]
    out_specs = [wide]
    scratch = []
    if with_image:
        args += far([other])
        specs.append(wide)
        cols = width // RADIX
        split = (RADIX // 2, part, cols)
        outs += [jax.ShapeDtypeStruct(split, F32)] * 2
        out_specs += [whole(split)] * 2
        scratch = [pltpu.VMEM((part, width), F32)]
    alias = {}
    if held is not None:
        alias = {3 + len(args): 0}
        args += far([held])
        specs.append(ANY)
    args += far(after)
    specs += [ANY] * len(after)
    got = pl.pallas_call(
        lambda *refs: last_kernel(with_image, *refs),
        grid_spec=pltpu.PrefetchScalarGridSpec(
            num_scalar_prefetch=3,
            grid=(1,),
            in_specs=specs,
            out_specs=out_specs,
            scratch_shapes=scratch,
        ),
        out_shape=outs,
        input_output_aliases=alias,
        compiler_params=params(),
        cost_estimate=LONG,
        name="along_y_last_r" if with_image else "along_y_last_s",
    )(shift, slot, place, *args)
    return got[0], got[1:]


def cut_kernel(shift_ref, shot_ref, place_ref, owner_ref, slab_ref, *outs):
    part, block = outs[0].shape[1:]
    for t in range(RADIX):
        row = 2 * lax.rem(place_ref[0] + t, RADIX) + shot_ref[0]
        rows = pl.ds(pl.multiple_of(row * part, part), part)
        for s in range(RADIX):
            cols = pl.ds(pl.multiple_of(block_of(shift_ref[0], s) * block, block), block)
            outs[s][t] = slab_ref[0, rows, cols]
    kept = (owner_ref[NZ - 1] == place_ref[0]).astype(F32)
    half = outs[-1].shape[0]
    outs[-1][...] = slab_ref[0, pl.ds(pl.multiple_of(shot_ref[0] * half, half), half), :] * kept


def cut_stage(slowness, shift, shot, place, owner):
    _, rows, width = slowness.shape
    outs = [(RADIX, rows // (2 * RADIX), width // RADIX)] * RADIX + [(rows // 2, width)]
    got = pl.pallas_call(
        cut_kernel,
        grid_spec=pltpu.PrefetchScalarGridSpec(
            num_scalar_prefetch=4,
            grid=(1,),
            in_specs=[whole(slowness.shape)],
            out_specs=[whole(o) for o in outs],
        ),
        out_shape=[jax.ShapeDtypeStruct(o, F32) for o in outs],
        compiler_params=params(),
        cost_estimate=LONG,
        name="cut_slab",
    )(shift, shot, place, owner, slowness)
    return got[:RADIX], got[RADIX]


def regroup_kernel(*refs):
    ins, outs = refs[:RADIX], refs[-RADIX:]
    for t in range(RADIX):
        for s in range(RADIX):
            outs[t][s] = ins[s][t]


def regroup_stage(pieces, after):
    shape = pieces[0].shape
    return pl.pallas_call(
        regroup_kernel,
        grid=(1,),
        in_specs=[whole(shape)] * RADIX + [ANY],
        out_specs=[whole(shape)] * RADIX,
        out_shape=[jax.ShapeDtypeStruct(shape, F32)] * RADIX,
        compiler_params=params(),
        cost_estimate=LONG,
        name="regroup_slab",
    )(*far(pieces), after)


def choose_kernel(place_ref, owner_ref, *refs):
    pieces, out_ref = refs[:RADIX], refs[-1]
    at = lax.rem(owner_ref[0] - place_ref[0] + RADIX, RADIX)
    for t, piece in enumerate(pieces):

        @pl.when(at == t)
        def _():
            out_ref[...] = piece[...]


def choose_stage(pieces, place, owner, after):
    shape = pieces[0].shape
    return pl.pallas_call(
        choose_kernel,
        grid_spec=pltpu.PrefetchScalarGridSpec(
            num_scalar_prefetch=2,
            grid=(1,),
            in_specs=[whole(shape)] * RADIX + [ANY] * len(after),
            out_specs=whole(shape),
        ),
        out_shape=jax.ShapeDtypeStruct(shape, F32),
        compiler_params=params(),
        cost_estimate=LONG,
        name="choose_slab",
    )(place, owner, *pieces, *far(after))


def phase_kernel(slot_ref, place_ref, shot_ref, *refs):
    pieces, (cos_ref, sin_ref) = refs[: 2 * RADIX], refs[-2:]
    part = pieces[0].shape[1]
    omega = omega_of(slot_ref[0])
    for n, piece in enumerate(pieces):
        t, other = n % RADIX, n // RADIX
        shot = shot_ref[0] if other == 0 else 1 - shot_ref[0]
        row = 2 * lax.rem(place_ref[0] + t, RADIX) + shot
        at = pl.ds(pl.multiple_of(row * part, part), part)
        for s in range(RADIX):
            theta = omega * (piece[s] - ref_slow) * dz_km
            cos_ref[s, at, :], sin_ref[s, at, :] = phase_parts(theta)


def phase_stage(pieces, slot, place, shot, after):
    _, part, cols = pieces[0].shape
    shape = (RADIX, part * len(pieces), cols)
    return pl.pallas_call(
        phase_kernel,
        grid_spec=pltpu.PrefetchScalarGridSpec(
            num_scalar_prefetch=3,
            grid=(1,),
            in_specs=[whole(p.shape) for p in pieces] + [ANY],
            out_specs=[whole(shape)] * 2,
        ),
        out_shape=[jax.ShapeDtypeStruct(shape, F32)] * 2,
        compiler_params=params(),
        cost_estimate=BRIEF,
        name="phases",
    )(slot, place, shot, *pieces, after)


def add_kernel(a_ref, b_ref, *refs):
    refs[-1][...] = a_ref[...] + b_ref[...]


def add_stage(a, b, name, after=()):
    return pl.pallas_call(
        add_kernel,
        grid=(1,),
        in_specs=[whole(a.shape)] * 2 + [ANY] * len(after),
        out_specs=whole(a.shape),
        out_shape=jax.ShapeDtypeStruct(a.shape, F32),
        compiler_params=params(),
        cost_estimate=BRIEF,
        name=name,
    )(a, b, *far(after))


def fold_kernel(place_ref, a_ref, b_ref, keep_ref, send_ref):
    mine = lax.shift_right_logical(place_ref[0], 1)
    keep_ref[...] = a_ref[mine] + b_ref[mine]
    send_ref[...] = a_ref[1 - mine] + b_ref[1 - mine]


def fold_stage(a, b, place):
    shape = a.shape[1:]
    return pl.pallas_call(
        fold_kernel,
        grid_spec=pltpu.PrefetchScalarGridSpec(
            num_scalar_prefetch=1,
            grid=(1,),
            in_specs=[whole(a.shape)] * 2,
            out_specs=[whole(shape)] * 2,
        ),
        out_shape=[jax.ShapeDtypeStruct(shape, F32)] * 2,
        compiler_params=params(),
        cost_estimate=BRIEF,
        name="image_fold",
    )(place, a, b)


def join_kernel(shot_ref, a_ref, b_ref, out_ref):
    half = a_ref.shape[0]
    out_ref[pl.ds(pl.multiple_of(shot_ref[0] * half, half), half), :] = a_ref[...]
    out_ref[pl.ds(pl.multiple_of((1 - shot_ref[0]) * half, half), half), :] = b_ref[...]


def join_stage(a, b, shot):
    shape = (2 * a.shape[0], a.shape[1])
    return pl.pallas_call(
        join_kernel,
        grid_spec=pltpu.PrefetchScalarGridSpec(
            num_scalar_prefetch=1,
            grid=(1,),
            in_specs=[whole(a.shape)] * 2,
            out_specs=whole(shape),
        ),
        out_shape=jax.ShapeDtypeStruct(shape, F32),
        compiler_params=params(),
        cost_estimate=BRIEF,
        name="late_join",
    )(shot, a, b)


def image_kernel(chunks, early_ref, *refs):
    out_ref = refs[-1]
    count = (len(refs) - 1) // chunks
    out_ref[0] = early_ref[...]
    part = refs[0].shape[0]
    for c in range(chunks):
        mine = refs[c * count : (c + 1) * count]
        total = mine[0][...]
        for ref in mine[1:]:
            total = total + ref[...]
        out_ref[1, pl.ds(c * part, part), :] = total


def image_stage(early, groups):
    rows, cols = early.shape
    args = [early] + [piece for group in groups for piece in group]
    return pl.pallas_call(
        lambda *refs: image_kernel(len(groups), *refs),
        out_shape=jax.ShapeDtypeStruct((NZ, rows, cols), F32),
        compiler_params=params(),
        cost_estimate=LONG,
        name="image_sum",
    )(*args)


def shifted(value, axis, step):
    count = lax.axis_size(axis)
    return lax.ppermute(value, axis, [((i + step) % count, i) for i in range(count)])


def swap_slots(pieces, axis):
    count = len(pieces)
    sent = [lax.ppermute(pieces[s], axis, [(i, (i + s) % count) for i in range(count)]) for s in range(1, count)]
    return [pieces[0]] + [sent[count - s - 1] for s in range(1, count)]


def paired(value, axis, bits):
    return lax.ppermute(value, axis, [(i, i ^ bits) for i in range(lax.axis_size(axis))])


def swap_pairs(pieces, axis):
    count = len(pieces)
    return [pieces[0]] + [
        lax.ppermute(pieces[s], axis, [(i, i ^ s) for i in range(count)]) for s in range(1, count)
    ]


def gather_slots(piece, axis):
    return [piece] + [shifted(piece, axis, s) for s in range(1, lax.axis_size(axis))]


CHUNKS = 2


def body(source_field, receiver_field, slowness, owner, freq_index):
    rows, width = source_field.shape[2:]
    row_count = lax.axis_size("row")
    freq_count = lax.axis_size("freq")
    row_at = lax.axis_index("row")
    place = lax.axis_index("freq")[None]
    shot = lax.axis_index("shot")[None]
    slot = freq_index
    ringed = row_count == RADIX and freq_count == RADIX and slowness.shape[0] == 1
    ringed = ringed and lax.axis_size("shot") == 2
    shift = row_at[None] if ringed else jnp.zeros((1,), jnp.int32)
    if not ringed:
        return general(source_field, receiver_field, slowness, owner, slot, shift, place)

    turned, late = cut_stage(slowness, shift, shot, place, owner)
    turned = swap_pairs(turned, "row")
    late = add_stage(late, paired(late, "freq", 2), "late_first")
    s_first, blocks = first_stage(source_field, shift, slot, None, 2, (turned[0],))
    s_mid = swap_pairs(s_first, "row")
    r_first, _ = first_stage(receiver_field, shift, slot, blocks, 2, turned[1:])
    r_mid = swap_pairs(r_first, "row")
    shares = swap_slots(regroup_stage(turned, r_first[0]), "freq")
    gathered = gather_slots(choose_stage(shares, place, owner, [s_mid[2], r_mid[2], late]), "freq")
    gathered += [lax.ppermute(g, "shot", [(0, 1), (1, 0)]) for g in gathered]
    s_half = half_stage(s_mid, blocks, shift)
    phases = phase_stage(gathered, slot, place, shot, s_half)

    s_pieces, s_held = middle_stage([s_half], phases, blocks, shift, place, 1, None, r_mid[1:])
    s_last = swap_pairs(s_pieces[0], "row")
    late_total = add_stage(late, paired(late, "freq", 1), "late_second")
    r_pieces, term = middle_stage(r_mid, phases, blocks, shift, place, CHUNKS, s_held)
    r_last = [swap_pairs(p, "row") for p in r_pieces]
    late = join_stage(late_total, paired(late_total, "shot", 1), shot)
    keep, send = fold_stage(term[0], paired(term[1], "freq", 1), place)
    total = add_stage(keep, paired(send, "freq", 2), "first_image")
    pairs = []
    for r in range(RADIX):
        for f in range(RADIX):
            pairs.append((r * RADIX + f, (r ^ f) * RADIX + r))

    source_out, _ = last_stage(s_last, late, blocks, shift, slot, place, 0, rows, None, None)
    receiver_out, groups = None, []
    for c in range(CHUNKS):
        receiver_out, terms = last_stage(
            r_last[c], late, blocks, shift, slot, place, c * (rows // CHUNKS), rows, source_out, receiver_out,
            [total] if c == CHUNKS - 1 else [],
        )
        part_keep, part_send = fold_stage(terms[0], paired(terms[1], "freq", 1), place)
        groups.append([part_keep, paired(part_send, "freq", 2)])
    first_image = lax.ppermute(total, ("row", "freq"), pairs)
    return (source_out, receiver_out, image_stage(first_image, groups))


def general(source_field, receiver_field, slowness, owner, slot, shift, place):
    rows, width = source_field.shape[2:]
    slab_dev = slowness.shape[0]
    slabs = []
    for depth in range(NZ):
        chosen = owner[depth]
        kept = lax.dynamic_index_in_dim(slowness, chosen % slab_dev, 0, keepdims=False)
        slabs.append(lax.psum(jnp.where(place[0] == chosen // slab_dev, kept, 0.0), "freq"))
    s_first, blocks = first_stage(source_field, shift, slot, None, 1)
    r_first, _ = first_stage(receiver_field, shift, slot, blocks, 1)

    def to_columns(pieces):
        whole_rows = jnp.concatenate(pieces, axis=2)
        return lax.all_to_all(whole_rows, "row", split_axis=2, concat_axis=1, tiled=True)

    def to_rows(pieces):
        whole_cols = jnp.concatenate(pieces, axis=1)
        return lax.all_to_all(whole_cols, "row", split_axis=1, concat_axis=2, tiled=True)

    s_mid = jnp.split(to_columns(s_first), RADIX, axis=1)
    r_mid = jnp.split(to_columns(r_first), RADIX, axis=1)
    turned = lax.all_to_all(slabs[0], "row", split_axis=1, concat_axis=0, tiled=True)
    theta = omega_of(slot[0]) * (turned - ref_slow) * dz_km
    theta = theta.reshape(RADIX, -1, theta.shape[1])
    phases = (jnp.cos(theta), jnp.sin(theta))
    s_pieces, s_held = middle_stage([half_stage(s_mid, blocks, shift)], phases, blocks, shift, shift, 1, None)
    r_pieces, term = middle_stage(r_mid, phases, blocks, shift, shift, 1, s_held)
    s_last = jnp.split(to_rows(s_pieces[0]), RADIX, axis=2)
    r_last = jnp.split(to_rows(r_pieces[0]), RADIX, axis=2)
    source_out, _ = last_stage(s_last, slabs[1], blocks, shift, slot, shift, 0, rows, None, None)
    receiver_out, terms = last_stage(
        r_last, slabs[1], blocks, shift, slot, shift, 0, rows, source_out, None
    )
    term = jnp.stack([term[0][0], term[1][0], term[0][1], term[1][1]]).reshape(-1, term[0].shape[2])
    images = [lax.all_to_all(term, "row", split_axis=0, concat_axis=1, tiled=True)]
    images.append(jnp.concatenate([terms[0][0], terms[1][0], terms[0][1], terms[1][1]], axis=1))
    parts = [lax.psum_scatter(t, "freq", scatter_dimension=1, tiled=True) for t in images]
    return (source_out, receiver_out, jnp.stack(parts))


def solution(mesh):
    in_specs = (
        P(None, ("shot", "freq"), "row", None),
        P(None, ("shot", "freq"), "row", None),
        P("freq", "row", None),
        P(),
        P(("shot", "freq")),
    )
    out_specs = (
        P(None, ("shot", "freq"), "row", None),
        P(None, ("shot", "freq"), "row", None),
        P("shot", "row", "freq"),
    )
    return jax.shard_map(body, mesh=mesh, in_specs=in_specs, out_specs=out_specs, check_vma=False)
```
